32 devices in a mesh: dp: 8 (over z, y), fsdp: 4 (over x, core).
Axes of the slice: x: 2, y: 2, z: 4, core: 2. Of those that a mesh axis runs over, the one named last changes fastest.
Arguments:
- tokens: bfloat16 [8192, 768], P(('dp', 'fsdp')), may hold values from -6 to 6
- segment: int32 [8192], P(('dp', 'fsdp')), may hold values from 0 to 3, as said below
- buckets: int32 [2047], replicated, may hold values from 0 to 31
- routes: int32 [8192, 1], P(('dp', 'fsdp')), may hold values from 0 to 3; in each aligned block of 256 rows (0 to 255, 256 to 511, ...) at most 128 rows name the same one
- w_query: bfloat16 [768, 768], P(('dp', 'fsdp')), may hold values from -0.0546875 to 0.0546875
- w_key: bfloat16 [768, 768], P(('dp', 'fsdp')), may hold values from -0.21875 to 0.21875
- w_value: bfloat16 [768, 768], P(('dp', 'fsdp')), may hold values from -0.21875 to 0.21875
- w_output: bfloat16 [768, 768], P(('dp', 'fsdp')), may hold values from -1.75 to 1.75
- w_router: bfloat16 [768, 4], P(('dp', 'fsdp')), may hold values from -0.15625 to 0.15625
- norm_attn: bfloat16 [768], P(('dp', 'fsdp')), may hold values from 0.5 to 1.5
- norm_ffn: bfloat16 [768], P(('dp', 'fsdp')), may hold values from 0.5 to 1.5
- bias_table: bfloat16 [32, 12], replicated, may hold values from -4 to 4
- expert_in: bfloat16 [4, 768, 3072], P('fsdp', None, 'dp'), may hold values from -0.21875 to 0.21875
- expert_out: bfloat16 [4, 3072, 768], P('fsdp', 'dp'), may hold values from -0.75 to 0.75
- out_grad: bfloat16 [8192, 768], P(('dp', 'fsdp')), may hold values from -6 to 6
Outputs:
- mixed: bfloat16 [8192, 768], P(('dp', 'fsdp'))
- d_tokens: bfloat16 [8192, 768], P(('dp', 'fsdp'))
- d_w_query: float32 [768, 768], P(('dp', 'fsdp'))
- d_w_key: float32 [768, 768], P(('dp', 'fsdp'))
- d_w_value: float32 [768, 768], P(('dp', 'fsdp'))
- d_w_output: float32 [768, 768], P(('dp', 'fsdp'))
- d_w_router: float32 [768, 4], P(('dp', 'fsdp'))
- d_norm_attn: float32 [768], P(('dp', 'fsdp'))
- d_norm_ffn: float32 [768], P(('dp', 'fsdp'))
- d_bias_table: float32 [32, 12], replicated
- d_expert_in: float32 [4, 768, 3072], P('fsdp', None, 'dp')
- d_expert_out: float32 [4, 3072, 768], P('fsdp', 'dp')
The draws below stay inside these ranges and needn't reach their ends.
Inputs may be any that keep to these rules, and one draw needn't show every extreme that they name: `segment`: within each group of 1024 consecutive tokens the ids never fall and start at 0; each id 0 to 3 holds at least one token of each group. `routes`: at most 128 of the rows of one device name the same expert.
All inputs are finite; a program needn't handle non-finite values.
Results may differ from the reference program's by a relative error of at most 0.02.
Values may be sent and summed in bfloat16 or wider, within the bound.
No kernel may reach another device: no remote copies, remote signals or barrier semaphores. Data moves between devices by JAX's collectives and lax.ppermute only.
A program may use at most 128 MiB of HBM per device.

```python
import math
import jax
import jax.numpy as jnp
import numpy as np
from jax import lax

D = 768
HEADS = 12
HEAD = 64
FF = 3072
BUCKETS = 32
TOK_DEV = 256
SEQS = 4
EXPERTS = 4
GROUP = 1024
TOKENS = 8192
CAP = 128
OFFSETS = 2047


def draw_segment(key, part):
    key = jax.random.fold_in(key, 11)
    groups = TOKENS // GROUP
    first_key, second_key = jax.random.split(key)
    longest = jax.random.randint(first_key, (groups, 1), 0, SEQS)
    shorter = jax.random.randint(second_key, (groups, SEQS), 1, TOK_DEV // SEQS + 1)
    order = jnp.arange(SEQS, dtype=jnp.int32)[None, :]
    shorter = jnp.where(order == longest, 0, shorter)
    lengths = jnp.where(order == longest, GROUP - jnp.sum(shorter, axis=1, keepdims=True), shorter)
    ends = jnp.cumsum(lengths, axis=1)[:, :-1]
    places = jnp.arange(GROUP, dtype=jnp.int32)
    ident = jnp.sum((places[None, :, None] >= ends[:, None, :]).astype(jnp.int32), axis=2)
    return ident.reshape(TOKENS).astype(jnp.int32)


def with_ends(values, rng, smallest, top_value):
    extent = values.shape
    spot = [jax.random.randint(jax.random.fold_in(rng, axis), (), 0, extent[axis]) for axis in range(len(extent))]
    values = values.at[tuple(spot)].set(smallest)
    longest = extent.index(max(extent))
    spot[longest] = (spot[longest] + 1) % extent[longest]
    return values.at[tuple(spot)].set(top_value)


def block_levels(rng, shape, pieces, smallest, largest):
    level = 1.0
    for dim, shards_of in pieces:
        draws = jax.random.uniform(jax.random.fold_in(jax.random.fold_in(rng, 6), dim), (shards_of,), jnp.float32, smallest / len(pieces), largest / len(pieces))
        level = level * jnp.repeat(jnp.exp(draws), shape[dim] // shards_of).reshape((-1,) + (1,) * (len(shape) - 1 - dim))
    return level


def shared_out(own_key, own, number, rows, count, top, reach, lean):
    order = jax.random.permutation(own_key, count)
    heavy_load, usual = load_shares(count, rows * top, reach, lean, True), load_shares(count, rows * top, reach, lean, False)
    places = jnp.arange(count)

    def named(sizes, offset_by):
        used = int((sizes > 0).sum())
        fixed = max(1, used // 4)
        shifted = fixed + (places - fixed + offset_by * (used - fixed)) % max(1, count - fixed)
        return jnp.zeros((count,), jnp.int32).at[order[jnp.where(places < fixed, places, shifted)]].set(jnp.asarray(sizes, jnp.int32))

    sizes = jnp.where(number % 4 == 0, named(heavy_load, number // 4), named(usual, number - number // 4 - 1))
    mixed = jax.random.permutation(jax.random.fold_in(own, 3), count)
    source_of, taker = mixed[0:count // 2 * 2:2], mixed[1:count // 2 * 2:2]
    slack = jnp.minimum(sizes[source_of] - 1, reach - sizes[taker]) // 2
    slack = jnp.where((source_of == order[0]) | (taker == order[0]) | (sizes[taker] == 0), 0, jnp.maximum(slack, 0))
    shifted = jax.random.randint(jax.random.fold_in(own, 4), (count // 2,), 0, 1 << 20) % (slack + 1)
    sizes = sizes.at[source_of].add(-shifted).at[taker].add(shifted)
    items = jnp.searchsorted(jnp.cumsum(sizes), jnp.arange(rows * top), side="right").astype(jnp.int32)
    table = items.reshape(top, rows).T
    table = table[jax.random.permutation(jax.random.fold_in(own, 1), rows)]
    offset_by = jax.random.randint(jax.random.fold_in(own, 2), (rows, 1), 0, top)
    return jnp.take_along_axis(table, (jnp.arange(top)[None, :] + offset_by) % top, axis=1)


def load_shares(amount, total, most, slope, full):
    loads = [(1 << 20) // math.isqrt(grade ** slope) + 1 for grade in range(1, amount + 1)]
    largest = most if full else min(most, max(-(-total // amount), total * loads[0] // sum(loads)))
    least = 1 if total - largest >= amount - 1 else 0
    holding, rest = [largest] + [least] * (amount - 1), total - largest - least * (amount - 1)
    while rest > 0:
        free = [i for i in range(1, amount) if holding[i] < largest] or [i for i in range(1, amount) if holding[i] < most]
        pool, left = sum([loads[i] for i in free]), rest
        for i in free:
            more = min(most - holding[i], max(1, left * loads[i] // pool), rest)
            holding[i] = holding[i] + more
            rest = rest - more
    return np.array(holding)


def gaussian(key, extent, deviation, limit, cuts=(), kind=jnp.bfloat16):
    entries = deviation * jax.random.normal(key, extent, jnp.float32)
    if cuts:
        entries = entries * block_levels(key, extent, cuts, -0.22, 0.18)
    return jnp.clip(entries, -limit, limit).astype(kind)


def setup_inputs(seed: int = 0) -> dict:
    arg_keys = jax.random.split(jax.random.key(seed), 16)
    tokens = gaussian(arg_keys[0], (TOKENS, D), 1.0, 6.0, ((0, 32),))
    segment = draw_segment(jax.random.fold_in(arg_keys[15], 71), 0)
    buckets = with_ends(jax.random.randint(arg_keys[2], (OFFSETS,), 0, BUCKETS), jax.random.fold_in(arg_keys[2], 1), 0, BUCKETS - 1).astype(jnp.int32)
    routes_keys = jax.random.split(jax.random.fold_in(arg_keys[3], 1), TOKENS // TOK_DEV)
    routes_turns = jax.random.permutation(jax.random.fold_in(arg_keys[3], 3), TOKENS // TOK_DEV)
    routes = jax.vmap(lambda own, number: shared_out(jax.random.fold_in(arg_keys[3], 2), own, number, TOK_DEV, EXPERTS, 1, CAP, 2))(routes_keys, routes_turns).reshape((TOKENS, 1))
    w_query = gaussian(arg_keys[4], (D, D), (16 * D) ** -0.5, 0.0546875, ((0, 32),))
    w_key = gaussian(arg_keys[5], (D, D), D ** -0.5, 0.21875, ((0, 32),))
    w_value = gaussian(arg_keys[6], (D, D), D ** -0.5, 0.21875, ((0, 32),))
    w_output = gaussian(arg_keys[7], (D, D), (D // 64) ** -0.5, 1.75, ((0, 32),))
    w_router = gaussian(arg_keys[8], (D, EXPERTS), (2 * D) ** -0.5, 0.15625, ((0, 32),))
    norm_attn = jnp.clip(1.0 + 0.1 * jax.random.normal(arg_keys[9], (D,), jnp.float32), 0.5, 1.5).astype(jnp.bfloat16)
    norm_ffn = jnp.clip(1.0 + 0.1 * jax.random.normal(arg_keys[10], (D,), jnp.float32), 0.5, 1.5).astype(jnp.bfloat16)
    bias_table = gaussian(arg_keys[11], (BUCKETS, HEADS), 1.0, 4.0)
    expert_in = gaussian(arg_keys[12], (EXPERTS, D, FF), D ** -0.5, 0.21875, ((0, 4), (2, 8)))
    expert_out = gaussian(arg_keys[13], (EXPERTS, FF, D), (max(1, FF // (3 * EXPERTS * EXPERTS))) ** -0.5, 0.75, ((0, 4), (1, 8)))
    out_grad = gaussian(arg_keys[14], (TOKENS, D), 1.0, 6.0, ((0, 32),))
    return dict(tokens=tokens, segment=segment, buckets=buckets, routes=routes, w_query=w_query, w_key=w_key, w_value=w_value, w_output=w_output, w_router=w_router, norm_attn=norm_attn, norm_ffn=norm_ffn, bias_table=bias_table, expert_in=expert_in, expert_out=expert_out, out_grad=out_grad)


EPSILON = 1e-06
MASKED = -1000000000.0
HIGHEST = lax.Precision.HIGHEST

@jax.custom_vjp
def low(v):
    return lax.optimization_barrier(v.astype(jnp.bfloat16)).astype(jnp.float32)

@jax.custom_vjp
def low_back(v):
    return v

def low_keep(v):
    return (low(v), None)

def low_pass(kept, grad):
    return (grad,)

def back_keep(v):
    return (v, None)

def back_low(kept, grad):
    return (low(grad),)
low.defvjp(low_keep, low_pass)
low_back.defvjp(back_keep, back_low)

def rounded(values):
    return low_back(low(values))

def matmul(left, right):
    return jnp.dot(left, right, precision=HIGHEST, preferred_element_type=jnp.float32)

def normalize(values, scale):
    return values * lax.rsqrt(lax.optimization_barrier(jnp.mean(values * values, axis=-1, keepdims=True)) + EPSILON) * scale

def reference(tokens, segment, buckets, routes, w_query, w_key, w_value, w_output, w_router, norm_attn, norm_ffn, bias_table, expert_in, expert_out, out_grad):
    groups = TOKENS // GROUP
    shards = TOKENS // TOK_DEV
    query_block = math.gcd(GROUP, 512)
    blocks = GROUP // query_block
    places = jnp.arange(GROUP, dtype=jnp.int32)
    starts = jnp.arange(blocks, dtype=jnp.int32) * query_block
    seg_groups = segment.reshape(groups, GROUP)
    bucket_hot = (buckets[:, None] == jnp.arange(BUCKETS, dtype=jnp.int32)[None, :]).astype(jnp.float32)
    route = routes[:, 0]
    picked = (route[:, None] == jnp.arange(EXPERTS, dtype=jnp.int32)[None, :]).astype(jnp.int32)
    picked_shards = picked.reshape(shards, TOK_DEV, EXPERTS)
    rank = lax.optimization_barrier(jnp.sum((jnp.cumsum(picked_shards, axis=1) - 1) * picked_shards, axis=2))
    slot = (route.reshape(shards, TOK_DEV) * CAP + rank).astype(jnp.int32)
    shard_rows = jnp.arange(shards, dtype=jnp.int32)[:, None]
    local_rows = jnp.broadcast_to(jnp.arange(TOK_DEV, dtype=jnp.int32)[None, :], (shards, TOK_DEV))
    source = jnp.zeros((shards, EXPERTS * CAP), jnp.int32).at[shard_rows, slot].set(local_rows)
    filled = jnp.zeros((shards, EXPERTS * CAP), jnp.float32).at[shard_rows, slot].set(1.0)
    picked_float = picked.astype(jnp.float32)

    def forward(inputs, weight_query, weight_key, weight_value, weight_output, weight_router, gain_attn, gain_ffn, bias_lookup, weight_in, weight_out):
        hidden = low(normalize(inputs, gain_attn))
        queries = rounded(matmul(hidden, weight_query))
        keys = rounded(matmul(hidden, weight_key))
        values = rounded(matmul(hidden, weight_value))
        offsets = matmul(bucket_hot, bias_lookup).T

        def attend_group(group_args):
            group_queries, group_keys, group_values, seg_all = group_args
            key_heads = group_keys.reshape(GROUP, HEADS, HEAD)
            head_values = group_values.reshape(GROUP, HEADS, HEAD)
            query_heads = group_queries.reshape(blocks, query_block, HEADS, HEAD)

            def attend_block(block_args):
                query_part, start = block_args
                query_pos = start + jnp.arange(query_block, dtype=jnp.int32)
                index = places[None, :] - query_pos[:, None] + (GROUP - 1)
                scores = jnp.einsum('qhe,khe->hqk', query_part, key_heads, precision=HIGHEST) + offsets[:, index]
                query_seg = lax.dynamic_slice_in_dim(seg_all, start, query_block)
                keep = query_seg[:, None] == seg_all[None, :]
                scores = jnp.where(keep[None], low_back(scores), MASKED)
                weights = low(jax.nn.softmax(scores, axis=-1))
                return jnp.einsum('hqk,khe->qhe', weights, head_values, precision=HIGHEST)
            attended = lax.map(jax.checkpoint(attend_block), (query_heads, starts))
            return attended.reshape(GROUP, D)
        attended = lax.map(attend_group, (queries.reshape(groups, GROUP, D), keys.reshape(groups, GROUP, D), values.reshape(groups, GROUP, D), seg_groups))
        attn_out = rounded(attended.reshape(TOKENS, D))
        residual = inputs + low_back(matmul(attn_out, weight_output))
        hidden2 = low(normalize(residual, gain_ffn))
        logits = low_back(matmul(hidden2, weight_router))
        gate = lax.optimization_barrier(jnp.sum(jax.nn.softmax(logits, axis=-1) * picked_float, axis=-1))
        hidden_shards = hidden2.reshape(shards, TOK_DEV, D)
        expert_rows = jnp.take_along_axis(hidden_shards, source[:, :, None], axis=1) * filled[:, :, None]
        expert_rows = jnp.transpose(expert_rows.reshape(shards, EXPERTS, CAP, D), (1, 0, 2, 3)).reshape(EXPERTS, shards * CAP, D)

        def expert_apply(expert_args):
            rows_in, inner, outer = expert_args
            pre = low_back(matmul(rows_in, inner))
            act = low(jax.nn.gelu(pre, approximate=True))
            return rounded(matmul(act, outer))
        results = lax.map(jax.checkpoint(expert_apply), (expert_rows, weight_in, weight_out))
        results = jnp.transpose(results.reshape(EXPERTS, shards, CAP, D), (1, 0, 2, 3)).reshape(shards, EXPERTS * CAP, D)
        token_results = jnp.take_along_axis(results, slot[:, :, None], axis=1).reshape(TOKENS, D)
        return residual + gate[:, None] * token_results
    floats = [array.astype(jnp.float32) for array in (tokens, w_query, w_key, w_value, w_output, w_router, norm_attn, norm_ffn, bias_table, expert_in, expert_out)]
    mixed, pullback = jax.vjp(forward, floats[0], floats[1], floats[2], floats[3], floats[4], floats[5], floats[6], floats[7], floats[8], floats[9], floats[10])
    grads = pullback(out_grad.astype(jnp.float32))
    return (mixed.astype(jnp.bfloat16), grads[0].astype(jnp.bfloat16), grads[1], grads[2], grads[3], grads[4], grads[5], grads[6], grads[7], grads[8], grads[9], grads[10])
```

```python
import functools

import jax
import jax.numpy as jnp
from jax import lax
from jax.experimental import pallas as pl
from jax.experimental.pallas import tpu as pltpu
from jax.sharding import PartitionSpec as P

HEADS = 12
HEAD = 64
BUCKETS = 32
LANES = 128
SUBLANES = 8

EPSILON = 1e-06
MASKED = -1000000000.0
HIGHEST = lax.Precision.HIGHEST
BF16 = jnp.bfloat16
F32 = jnp.float32


def inverse_rms(values):
    return lax.rsqrt(jnp.mean(values * values, axis=-1, keepdims=True) + EPSILON)


def norm_gradient(grad, gain, unit, scale):
    inner = grad * gain
    return scale * (inner - unit * jnp.mean(inner * unit, axis=-1, keepdims=True))


def gelu_tanh(values):
    return jax.nn.gelu(values, approximate=True)


def product(left, right):
    return jnp.dot(left, right, preferred_element_type=F32)


def contract(left, left_dim, right, right_dim, precision=None):
    return lax.dot_general(
        left,
        right,
        (((left_dim,), (right_dim,)), ((), ())),
        precision=precision,
        preferred_element_type=F32,
    )


def attend_kernel(off_ref, seg_query_ref, seg_key_ref, q_ref, k_ref, v_ref, o_ref, p_ref, skew_ref):
    turn = pl.program_id(1)
    rows = q_ref.shape[1]
    group = k_ref.shape[1]
    width = skew_ref.shape[1]

    @pl.when(turn == 0)
    def _():
        wide = jnp.broadcast_to(off_ref[0], (LANES, width))
        skew_ref[...] = pltpu.roll(wide, width - (LANES - 1), 1, stride=1, stride_axis=0)

    scores = contract(q_ref[0], 1, k_ref[0], 1)
    for part in range(rows // LANES):
        here = slice(part * LANES, (part + 1) * LANES)
        start = group - LANES - turn * rows - part * LANES
        bias = skew_ref[:, pl.ds(pl.multiple_of(start, LANES), group)]
        keep = seg_query_ref[here, :] == seg_key_ref[...]
        biased = jnp.where(keep, scores[here] + bias, MASKED)
        top = jnp.max(biased, axis=1, keepdims=True)
        weights = jnp.exp(biased - top)
        total = jnp.sum(weights, axis=1, keepdims=True)
        probs = (weights * (1.0 / total)).astype(BF16)
        p_ref[0, here, :] = probs
        o_ref[0, here, :] = product(probs, v_ref[0]).astype(BF16)


def attend_back_kernel(
    p_ref, do_ref, q_ref, k_ref, v_ref, dq_ref, dk_ref, dv_ref, doff_ref, dk_acc, dv_acc, diag
):
    turn = pl.program_id(1)
    rows = q_ref.shape[1]
    group = k_ref.shape[1]
    width = diag.shape[1]

    @pl.when(turn == 0)
    def _():
        dk_acc[...] = jnp.zeros_like(dk_acc)
        dv_acc[...] = jnp.zeros_like(dv_acc)
        diag[...] = jnp.zeros_like(diag)

    probs = p_ref[0]
    grad = do_ref[0]
    grad_probs = contract(grad, 1, v_ref[0], 1)
    wide = probs.astype(F32)
    correction = jnp.sum(wide * grad_probs, axis=1, keepdims=True)
    grad_scores = (wide * (grad_probs - correction)).astype(BF16)
    dq_ref[0] = product(grad_scores, k_ref[0]).T.astype(BF16)
    dk_acc[...] += contract(q_ref[0], 0, grad_scores, 0)
    dv_acc[...] += contract(grad, 0, probs, 0)
    for part in range(rows // LANES):
        start = group - LANES - turn * rows - part * LANES
        there = pl.ds(pl.multiple_of(start, LANES), group)
        diag[:, there] += grad_scores[part * LANES : (part + 1) * LANES, :].astype(F32)

    @pl.when(turn == pl.num_programs(1) - 1)
    def _():
        dk_ref[0] = dk_acc[...].astype(BF16)
        dv_ref[0] = dv_acc[...].astype(BF16)
        lined = jnp.zeros((SUBLANES, width), F32)
        for first in range(0, LANES, SUBLANES):
            lined += pltpu.roll(diag[first : first + SUBLANES, :], LANES - 1 - first, 1)
        row = lax.broadcasted_iota(jnp.int32, lined.shape, 0)
        for bit in (1, 2, 4):
            lined = jnp.where((row & bit) != 0, pltpu.roll(lined, width - bit, 1), lined)
        doff_ref[0] = jnp.sum(lined, axis=0, keepdims=True)


VMEM_LIMIT = 50 * 1024 * 1024


def attend(offsets, segment, queries, keys, values):
    heads, group, size = queries.shape
    width = offsets.shape[-1]
    rows = min(256, group)
    one = pl.BlockSpec((1, group, size), lambda h, b: (h, 0, 0))
    block = pl.BlockSpec((1, rows, size), lambda h, b: (h, b, 0))
    return pl.pallas_call(
        attend_kernel,
        grid=(heads, group // rows),
        in_specs=[
            pl.BlockSpec((1, 1, width), lambda h, b: (h, 0, 0)),
            pl.BlockSpec((rows, 1), lambda h, b: (b, 0)),
            pl.BlockSpec((1, group), lambda h, b: (0, 0)),
            block,
            one,
            one,
        ],
        out_specs=[block, pl.BlockSpec((1, rows, group), lambda h, b: (h, b, 0))],
        out_shape=[
            jax.ShapeDtypeStruct((heads, group, size), BF16),
            jax.ShapeDtypeStruct((heads, group, group), BF16),
        ],
        scratch_shapes=[pltpu.VMEM((LANES, width), F32)],
        compiler_params=pltpu.CompilerParams(vmem_limit_bytes=VMEM_LIMIT),
        cost_estimate=pl.CostEstimate(
            flops=16 * heads * group * group * size,
            bytes_accessed=2 * heads * group * (group + 4 * size),
            transcendentals=heads * group * group,
        ),
        name="attend",
    )(offsets.reshape(heads, 1, width), segment[:, None], segment[None, :], queries, keys, values)


def attend_back(probs, grads, queries, keys, values, width):
    heads, group, size = queries.shape
    rows = min(256, group)
    one = pl.BlockSpec((1, group, size), lambda h, b: (h, 0, 0))
    block = pl.BlockSpec((1, rows, size), lambda h, b: (h, b, 0))
    across = pl.BlockSpec((1, size, group), lambda h, b: (h, 0, 0))
    turned = jax.ShapeDtypeStruct((heads, size, group), BF16)
    return pl.pallas_call(
        attend_back_kernel,
        grid=(heads, group // rows),
        in_specs=[
            pl.BlockSpec((1, rows, group), lambda h, b: (h, b, 0)),
            block,
            block,
            one,
            one,
        ],
        out_specs=[
            pl.BlockSpec((1, size, rows), lambda h, b: (h, 0, b)),
            across,
            across,
            pl.BlockSpec((1, 1, width), lambda h, b: (h, 0, 0)),
        ],
        out_shape=[
            turned,
            turned,
            turned,
            jax.ShapeDtypeStruct((heads, 1, width), F32),
        ],
        scratch_shapes=[
            pltpu.VMEM((size, group), F32),
            pltpu.VMEM((size, group), F32),
            pltpu.VMEM((LANES, width), F32),
        ],
        compiler_params=pltpu.CompilerParams(vmem_limit_bytes=VMEM_LIMIT),
        cost_estimate=pl.CostEstimate(
            flops=32 * heads * group * group * size,
            bytes_accessed=2 * heads * group * (group + 8 * size),
            transcendentals=0,
        ),
        name="attend_back",
    )(probs, grads, queries, keys, values)


def exchange(blocks):
    return lax.all_to_all(blocks, "fsdp", split_axis=0, concat_axis=0, tiled=True)


def total_everywhere(part):
    for axis in ("fsdp", "dp"):
        size = lax.axis_size(axis)
        step = 1
        while step < size:
            part = part + lax.ppermute(part, axis, [(i, i ^ step) for i in range(size)])
            step *= 2
    return part


def pad_lanes(array):
    short = -array.shape[-1] % LANES
    return jnp.pad(array, [(0, 0)] * (array.ndim - 1) + [(0, short)])


def body(
    tokens,
    segment,
    buckets,
    routes,
    w_query,
    w_key,
    w_value,
    w_output,
    w_router,
    norm_attn,
    norm_ffn,
    bias_table,
    expert_in,
    expert_out,
    out_grad,
):
    tok_rows, model = tokens.shape
    shard_rows = w_query.shape[0]
    peers = lax.axis_size("fsdp")
    group = tok_rows * peers
    capacity = 2 * tok_rows // peers
    heads = -(-HEADS // peers)
    own_cols = heads * HEAD
    all_cols = peers * own_cols
    me = lax.axis_index("fsdp")

    def by_peer(matrix):
        padded = jnp.pad(matrix, ((0, 0), (0, all_cols - HEADS * HEAD)))
        return jnp.transpose(padded.reshape(matrix.shape[0], peers, own_cols), (1, 0, 2))

    rest = jnp.concatenate([w_output, w_router, norm_attn[:, None], norm_ffn[:, None]], axis=1)
    packed = pad_lanes(
        jnp.concatenate(
            [
                by_peer(w_query),
                by_peer(w_key),
                by_peer(w_value),
                jnp.broadcast_to(rest[None], (peers,) + rest.shape),
            ],
            axis=2,
        )
    )
    dense = exchange(packed).reshape(peers * shard_rows, packed.shape[-1])
    dense = lax.all_gather(dense, "dp", axis=0, tiled=True)
    qkv_cols = 3 * own_cols
    weight_qkv = dense[:, :qkv_cols]
    weight_output = dense[:, qkv_cols : qkv_cols + model]
    weight_router = dense[:, qkv_cols + model : qkv_cols + model + peers]
    gains = dense[:, qkv_cols + model + peers : qkv_cols + model + peers + 2].astype(F32).T
    gain_attn, gain_ffn = gains[0:1], gains[1:2]

    tokens_all = lax.all_gather(tokens, "fsdp", axis=0, tiled=True)
    segment_all = lax.all_gather(segment, "fsdp", axis=0, tiled=True)

    ff_rows = expert_out.shape[1]
    expert_pack = jnp.concatenate([expert_in[0].T, expert_out[0]], axis=1)
    expert_all = lax.all_gather(expert_pack, "dp", axis=0, tiled=True)
    weight_in = expert_all[:, :model]
    weight_out = expert_all[:, model:]

    route = routes[:, 0]
    picked = (route[:, None] == jnp.arange(peers, dtype=jnp.int32)[None, :]).astype(jnp.int32)
    picked_float = picked.astype(F32)
    rank = jnp.sum((jnp.cumsum(picked, axis=0) - 1) * picked, axis=1)
    slot = route * capacity + rank
    slots = peers * capacity
    placing = (jnp.arange(slots, dtype=jnp.int32)[:, None] == slot[None, :]).astype(BF16)

    def dispatch(rows):
        placed = product(placing, rows).astype(BF16).reshape(peers, capacity, rows.shape[-1])
        return exchange(placed).reshape(slots, rows.shape[-1])

    def give_back(rows):
        returned = exchange(rows.reshape(peers, capacity, rows.shape[-1]))
        return contract(placing, 0, returned.reshape(slots, rows.shape[-1]), 0)

    grad_arrived = dispatch(out_grad)

    bucket_hot = (
        jnp.pad(buckets, (0, 1), constant_values=-1)[:, None]
        == jnp.arange(BUCKETS, dtype=jnp.int32)[None, :]
    )
    table_pad = jnp.pad(bias_table, ((0, 0), (0, peers * heads - HEADS)))
    own_table = lax.dynamic_slice_in_dim(table_pad, me * heads, heads, 1)
    offsets = contract(own_table, 0, bucket_hot.astype(BF16), 1)

    wide_all = tokens_all.astype(F32)
    unit_all = wide_all * inverse_rms(wide_all)
    hidden = (unit_all * gain_attn).astype(BF16)
    qkv = product(hidden, weight_qkv).astype(BF16)
    qkv = jnp.transpose(qkv.reshape(group, 3, heads, HEAD), (1, 2, 0, 3))
    queries, keys, values = qkv[0], qkv[1], qkv[2]
    attended, probs = attend(offsets, segment_all, queries, keys, values)
    blocks = jnp.transpose(attended, (1, 0, 2)).reshape(peers, tok_rows, own_cols)
    attn_out = jnp.transpose(exchange(blocks), (1, 0, 2)).reshape(tok_rows, all_cols)
    attn_out = attn_out[:, : HEADS * HEAD]

    inputs = tokens.astype(F32)
    residual = inputs + product(attn_out, weight_output)
    scale_ffn = inverse_rms(residual)
    unit_ffn = residual * scale_ffn
    hidden2 = (unit_ffn * gain_ffn).astype(BF16)
    logits = product(hidden2, weight_router)
    chances = jax.nn.softmax(logits, axis=-1)
    gate = jnp.sum(chances * picked_float, axis=-1, keepdims=True)

    gate_high = gate.astype(BF16)
    gate_low = (gate - gate_high.astype(F32)).astype(BF16)
    arrived = dispatch(pad_lanes(jnp.concatenate([hidden2, gate_high, gate_low], axis=1)))
    gate_slots = jnp.sum(arrived[:, model : model + 2].astype(F32), axis=1, keepdims=True)
    arrived = arrived[:, :model]
    d_arrived = (gate_slots * grad_arrived.astype(F32)).astype(BF16)
    pre = contract(arrived, 1, weight_in, 1)
    activated, gelu_back = jax.vjp(gelu_tanh, pre)
    activated = activated.astype(BF16)
    result = product(activated, weight_out).astype(BF16)
    token_result = give_back(result)
    d_activated = contract(d_arrived, 1, weight_out, 1)
    d_pre = gelu_back(d_activated)[0].astype(BF16)
    d_rows = product(d_pre, weight_in).astype(BF16)
    d_from_expert = give_back(d_rows)
    d_weight_out = contract(activated, 0, d_arrived, 0).astype(BF16)
    d_weight_in = contract(d_pre, 0, arrived, 0).astype(BF16)
    d_expert_out = lax.psum_scatter(d_weight_out, "dp", scatter_dimension=0, tiled=True)
    d_expert_in = lax.psum_scatter(d_weight_in, "dp", scatter_dimension=0, tiled=True)

    mixed = residual + gate * token_result
    grad_out = out_grad.astype(F32)
    d_gate = jnp.sum(grad_out * token_result, axis=-1, keepdims=True)
    d_logits = (gate * (picked_float - chances) * d_gate).astype(BF16)
    d_hidden2 = d_from_expert + contract(d_logits, 1, weight_router, 1)
    d_router = contract(hidden2, 0, d_logits, 0)
    d_gain_ffn = jnp.sum(d_hidden2 * unit_ffn, axis=0)
    d_residual = grad_out + norm_gradient(d_hidden2, gain_ffn, unit_ffn, scale_ffn)
    d_branch = d_residual.astype(BF16)
    d_weight_output = contract(attn_out, 0, d_branch, 0)
    d_attended = contract(d_branch, 1, weight_output, 1).astype(BF16)

    d_blocks = exchange(by_peer(d_attended)).reshape(group, heads, HEAD)
    d_heads = jnp.transpose(d_blocks, (1, 0, 2))
    d_queries, d_keys, d_values, d_offsets = attend_back(
        probs, d_heads, queries, keys, values, offsets.shape[-1]
    )
    d_table = contract(
        bucket_hot.astype(F32), 0, d_offsets.reshape(heads, offsets.shape[-1]), 1, HIGHEST
    )
    d_table = lax.dynamic_update_slice_in_dim(
        jnp.zeros((BUCKETS, peers * heads), F32), d_table, me * heads, 1
    )
    table_total = total_everywhere(d_table)[:, :HEADS]
    d_qkv = jnp.concatenate([d_queries, d_keys, d_values], axis=0).reshape(qkv_cols, group)
    d_hidden_part = contract(d_qkv, 0, weight_qkv, 1)
    d_gain_attn = jnp.sum(d_hidden_part * unit_all, axis=0)
    d_weight_qkv = contract(hidden, 0, d_qkv, 1)
    d_hidden = exchange(d_hidden_part.astype(BF16).reshape(peers, tok_rows, model))
    d_hidden = jnp.sum(d_hidden.astype(F32), axis=0)
    scale_attn = inverse_rms(inputs)
    d_inputs = d_residual + norm_gradient(d_hidden, gain_attn, inputs * scale_attn, scale_attn)

    def reduce_rows(matrix):
        part = lax.psum_scatter(pad_lanes(matrix.astype(BF16)), "dp", scatter_dimension=0, tiled=True)
        return exchange(part.reshape(peers, shard_rows, part.shape[-1])).astype(F32)

    rest_rows = reduce_rows(
        jnp.concatenate([d_weight_output, d_router, d_gain_ffn[:, None]], axis=1)
    )
    rest_rows = jnp.sum(rest_rows, axis=0)
    qkv_rows = reduce_rows(jnp.concatenate([d_weight_qkv, d_gain_attn[:, None]], axis=1))
    gain_attn_rows = jnp.sum(qkv_rows[:, :, qkv_cols], axis=0)

    def from_peers(turn):
        cols = qkv_rows[:, :, turn * own_cols : (turn + 1) * own_cols]
        return jnp.transpose(cols, (1, 0, 2)).reshape(shard_rows, all_cols)[:, : HEADS * HEAD]

    return (
        mixed.astype(BF16),
        d_inputs.astype(BF16),
        from_peers(0),
        from_peers(1),
        from_peers(2),
        rest_rows[:, :model],
        rest_rows[:, model : model + peers],
        gain_attn_rows,
        rest_rows[:, model + peers],
        table_total,
        d_expert_in.astype(F32).T[None],
        d_expert_out.astype(F32)[None],
    )


def solution(mesh):
    rows = P(("dp", "fsdp"), None)
    flat = P(("dp", "fsdp"))
    return jax.shard_map(
        body,
        mesh=mesh,
        in_specs=(
            rows,
            flat,
            P(),
            rows,
            rows,
            rows,
            rows,
            rows,
            rows,
            flat,
            flat,
            P(),
            P("fsdp", None, "dp"),
            P("fsdp", "dp", None),
            rows,
        ),
        out_specs=(
            rows,
            rows,
            rows,
            rows,
            rows,
            rows,
            rows,
            flat,
            flat,
            P(),
            P("fsdp", None, "dp"),
            P("fsdp", "dp", None),
        ),
        check_vma=False,
    )
```

```python
import functools

import jax
import jax.numpy as jnp
from jax import lax
from jax.experimental import pallas as pl
from jax.experimental.pallas import tpu as pltpu
from jax.sharding import PartitionSpec as P

HEADS = 12
HEAD = 64
BUCKETS = 32
LANES = 128
DP = ("z", "y")
EVERY = ("z", "y", "fsdp")
SUBLANES = 8

EPSILON = 1e-06
MASKED = -1000000000.0
HIGHEST = lax.Precision.HIGHEST
BF16 = jnp.bfloat16
F32 = jnp.float32


def inverse_rms(values):
    return lax.rsqrt(jnp.mean(values * values, axis=-1, keepdims=True) + EPSILON)


def norm_gradient(grad, gain, unit, scale):
    inner = grad * gain
    return scale * (inner - unit * jnp.mean(inner * unit, axis=-1, keepdims=True))


def product(left, right):
    return jnp.dot(left, right, preferred_element_type=F32)


def contract(left, left_dim, right, right_dim, precision=None):
    return lax.dot_general(
        left,
        right,
        (((left_dim,), (right_dim,)), ((), ())),
        precision=precision,
        preferred_element_type=F32,
    )


VMEM_LIMIT = 56 * 1024 * 1024


def head_slice(turn, heads, head):
    first = (turn * heads + head) * HEAD
    return slice(first, first + HEAD)


def attend_kernel(
    off_ref, seg_query_ref, seg_key_ref, hidden_ref, weight_ref, *refs, heads, waits
):
    qkv_ref, o_ref, p_ref, skew_ref = refs[waits:]
    turn = pl.program_id(0)
    rows = o_ref.shape[0]
    group = hidden_ref.shape[0]
    width = skew_ref.shape[2]

    @pl.when(turn == 0)
    def _():
        projected = product(hidden_ref[...], weight_ref[:, : 3 * heads * HEAD])
        qkv_ref[...] = projected.astype(BF16)
        for head in range(heads):
            wide = jnp.broadcast_to(off_ref[head : head + 1, :], (LANES, width))
            skew_ref[head] = pltpu.roll(wide, width - (LANES - 1), 1, stride=1, stride_axis=0)

    own_rows = pl.ds(pl.multiple_of(turn * rows, rows), rows)
    for head in range(heads):
        queries = qkv_ref[own_rows, head_slice(0, heads, head)]
        keys = qkv_ref[:, head_slice(1, heads, head)]
        values = qkv_ref[:, head_slice(2, heads, head)]
        scores = contract(queries, 1, keys, 1)
        for part in range(rows // LANES):
            here = slice(part * LANES, (part + 1) * LANES)
            start = group - LANES - turn * rows - part * LANES
            bias = skew_ref[head, :, pl.ds(pl.multiple_of(start, LANES), group)]
            keep = seg_query_ref[here, :] == seg_key_ref[...]
            biased = jnp.where(keep, scores[here] + bias, MASKED)
            top = jnp.max(biased, axis=1, keepdims=True)
            weights = jnp.exp(biased - top)
            total = jnp.sum(weights, axis=1, keepdims=True)
            probs = (weights * (1.0 / total)).astype(BF16)
            p_ref[head, here, :] = probs
            o_ref[here, head_slice(0, heads, head)] = product(probs, values).astype(BF16)


def attend_back_kernel(p_ref, do_ref, qkv_ref, *refs, heads, waits):
    dqkv_ref, doff_ref, dkv_acc, diag = refs[waits:]
    turn = pl.program_id(0)
    rows = do_ref.shape[0]
    group = qkv_ref.shape[0]
    width = diag.shape[2]

    @pl.when(turn == 0)
    def _():
        dkv_acc[...] = jnp.zeros_like(dkv_acc)
        diag[...] = jnp.zeros_like(diag)

    own_rows = pl.ds(pl.multiple_of(turn * rows, rows), rows)
    for head in range(heads):
        queries = qkv_ref[own_rows, head_slice(0, heads, head)]
        keys = qkv_ref[:, head_slice(1, heads, head)]
        values = qkv_ref[:, head_slice(2, heads, head)]
        probs = p_ref[head]
        grad = do_ref[:, head_slice(0, heads, head)]
        grad_probs = contract(grad, 1, values, 1)
        wide = probs.astype(F32)
        correction = jnp.sum(wide * grad_probs, axis=1, keepdims=True)
        grad_scores = (wide * (grad_probs - correction)).astype(BF16)
        dqkv_ref[head_slice(0, heads, head), own_rows] = product(grad_scores, keys).T.astype(BF16)
        dkv_acc[head_slice(0, heads, head), :] += contract(queries, 0, grad_scores, 0)
        dkv_acc[head_slice(1, heads, head), :] += contract(grad, 0, probs, 0)
        for part in range(rows // LANES):
            start = group - LANES - turn * rows - part * LANES
            there = pl.ds(pl.multiple_of(start, LANES), group)
            diag[head, :, there] += grad_scores[part * LANES : (part + 1) * LANES, :].astype(F32)

    @pl.when(turn == pl.num_programs(0) - 1)
    def _():
        dqkv_ref[heads * HEAD :, :] = dkv_acc[...].astype(BF16)
        for head in range(heads):
            lined = jnp.zeros((SUBLANES, width), F32)
            for first in range(0, LANES, SUBLANES):
                lined += pltpu.roll(diag[head, first : first + SUBLANES, :], LANES - 1 - first, 1)
            row = lax.broadcasted_iota(jnp.int32, lined.shape, 0)
            for bit in (1, 2, 4):
                lined = jnp.where((row & bit) != 0, pltpu.roll(lined, width - bit, 1), lined)
            doff_ref[head : head + 1, :] = jnp.sum(lined, axis=0, keepdims=True)


def whole_spec(array):
    return pl.BlockSpec(array.shape, lambda *_: (0,) * array.ndim)


def wait_specs(waits):
    return [pl.BlockSpec(memory_space=pl.ANY)] * len(waits)


def attend(offsets, segment, hidden, dense, waits):
    heads, width = offsets.shape
    group = hidden.shape[0]
    rows = min(256, group)
    own_cols = heads * HEAD
    operands = (offsets, segment[:, None], segment[None, :], hidden, dense)
    specs = [whole_spec(array) for array in operands]
    specs[1] = pl.BlockSpec((rows, 1), lambda b: (b, 0))
    return pl.pallas_call(
        functools.partial(attend_kernel, heads=heads, waits=len(waits)),
        grid=(group // rows,),
        in_specs=specs + wait_specs(waits),
        out_specs=[
            pl.BlockSpec((group, 3 * own_cols), lambda b: (0, 0)),
            pl.BlockSpec((rows, own_cols), lambda b: (b, 0)),
            pl.BlockSpec((heads, rows, group), lambda b: (0, b, 0)),
        ],
        out_shape=[
            jax.ShapeDtypeStruct((group, 3 * own_cols), BF16),
            jax.ShapeDtypeStruct((group, own_cols), BF16),
            jax.ShapeDtypeStruct((heads, group, group), BF16),
        ],
        scratch_shapes=[pltpu.VMEM((heads, LANES, width), F32)],
        compiler_params=pltpu.CompilerParams(vmem_limit_bytes=VMEM_LIMIT),
        cost_estimate=pl.CostEstimate(
            flops=16 * heads * group * group * HEAD,
            bytes_accessed=2 * heads * group * (group + 4 * HEAD),
            transcendentals=heads * group * group,
        ),
        name="attend",
    )(*operands, *waits)


def attend_back(probs, grads, qkv, width, waits):
    heads, group, _ = probs.shape
    rows = min(256, group)
    own_cols = heads * HEAD
    return pl.pallas_call(
        functools.partial(attend_back_kernel, heads=heads, waits=len(waits)),
        grid=(group // rows,),
        in_specs=[
            pl.BlockSpec((heads, rows, group), lambda b: (0, b, 0)),
            pl.BlockSpec((rows, own_cols), lambda b: (b, 0)),
            whole_spec(qkv),
        ]
        + wait_specs(waits),
        out_specs=[
            pl.BlockSpec((3 * own_cols, group), lambda b: (0, 0)),
            pl.BlockSpec((heads, width), lambda b: (0, 0)),
        ],
        out_shape=[
            jax.ShapeDtypeStruct((3 * own_cols, group), BF16),
            jax.ShapeDtypeStruct((heads, width), F32),
        ],
        scratch_shapes=[
            pltpu.VMEM((2 * own_cols, group), F32),
            pltpu.VMEM((heads, LANES, width), F32),
        ],
        compiler_params=pltpu.CompilerParams(vmem_limit_bytes=VMEM_LIMIT),
        cost_estimate=pl.CostEstimate(
            flops=32 * heads * group * group * HEAD,
            bytes_accessed=2 * heads * group * (group + 8 * HEAD),
            transcendentals=0,
        ),
        name="attend_back",
    )(probs, grads, qkv, *waits)


GELU_SLOPE = 0.7978845608028654
GELU_CUBE = 0.044715


def expert_kernel(rows_ref, weights_ref, result_ref, act_ref, slope_ref, acc):
    turn = pl.program_id(0)
    model = rows_ref.shape[1]

    @pl.when(turn == 0)
    def _():
        acc[...] = jnp.zeros_like(acc)

    pre = contract(rows_ref[...], 1, weights_ref[:, :model], 1)
    square = pre * pre
    bend = jnp.tanh(GELU_SLOPE * pre * (1.0 + GELU_CUBE * square))
    half = 0.5 * (1.0 + bend)
    activated = (pre * half).astype(BF16)
    slope = half + 0.5 * GELU_SLOPE * pre * (1.0 - bend * bend) * (1.0 + 3.0 * GELU_CUBE * square)
    act_ref[...] = activated
    slope_ref[...] = slope.astype(BF16)
    acc[...] += product(activated, weights_ref[:, model:])

    @pl.when(turn == pl.num_programs(0) - 1)
    def _():
        result_ref[...] = acc[...].astype(BF16)


def expert_back_kernel(
    rows_ref, grads_ref, weights_ref, act_ref, slope_ref, back_ref, dw_ref, acc
):
    turn = pl.program_id(0)
    model = rows_ref.shape[1]

    @pl.when(turn == 0)
    def _():
        acc[...] = jnp.zeros_like(acc)

    rows, grads = rows_ref[...], grads_ref[...]
    d_act = contract(grads, 1, weights_ref[:, model:], 1)
    d_pre = (slope_ref[...].astype(F32) * d_act).astype(BF16)
    acc[...] += product(d_pre, weights_ref[:, :model])
    dw_ref[:, :model] = contract(d_pre, 0, rows, 0).astype(BF16)
    dw_ref[:, model:] = contract(act_ref[...], 0, grads, 0).astype(BF16)

    @pl.when(turn == pl.num_programs(0) - 1)
    def _():
        back_ref[...] = acc[...].astype(BF16)


def expert_cost(slot_rows, model, units, products):
    return pl.CostEstimate(
        flops=2 * products * slot_rows * model * units,
        bytes_accessed=4 * units * (model + slot_rows),
        transcendentals=0,
    )


def run_expert(rows, weights):
    slot_rows, model = rows.shape
    units, width = weights.shape
    step = min(384, units)
    block = pl.BlockSpec((step, width), lambda i: (i, 0))
    across = pl.BlockSpec((slot_rows, step), lambda i: (0, i))
    hidden = jax.ShapeDtypeStruct((slot_rows, units), BF16)
    return pl.pallas_call(
        expert_kernel,
        grid=(units // step,),
        in_specs=[whole_spec(rows), block],
        out_specs=[whole_spec(rows), across, across],
        out_shape=[jax.ShapeDtypeStruct(rows.shape, BF16), hidden, hidden],
        scratch_shapes=[pltpu.VMEM(rows.shape, F32)],
        compiler_params=pltpu.CompilerParams(vmem_limit_bytes=VMEM_LIMIT),
        cost_estimate=expert_cost(slot_rows, model, units, 2),
        name="run_expert",
    )(rows, weights)


def run_expert_back(rows, grads, weights, activated, slopes):
    slot_rows, model = rows.shape
    units, width = weights.shape
    step = min(384, units)
    block = pl.BlockSpec((step, width), lambda i: (i, 0))
    across = pl.BlockSpec((slot_rows, step), lambda i: (0, i))
    return pl.pallas_call(
        expert_back_kernel,
        grid=(units // step,),
        in_specs=[whole_spec(rows), whole_spec(grads), block, across, across],
        out_specs=[whole_spec(rows), block],
        out_shape=[
            jax.ShapeDtypeStruct(rows.shape, BF16),
            jax.ShapeDtypeStruct((units, width), BF16),
        ],
        scratch_shapes=[pltpu.VMEM(rows.shape, F32)],
        compiler_params=pltpu.CompilerParams(vmem_limit_bytes=VMEM_LIMIT),
        cost_estimate=expert_cost(slot_rows, model, units, 4),
        name="run_expert_back",
    )(rows, grads, weights, activated, slopes)


def exchange(blocks):
    return lax.all_to_all(blocks, "fsdp", split_axis=0, concat_axis=0, tiled=True)


def total_everywhere(part):
    for axis in ("fsdp", "y", "z"):
        size = lax.axis_size(axis)
        step = 1
        while step < size:
            part = part + lax.ppermute(part, axis, [(i, i ^ step) for i in range(size)])
            step *= 2
    return part


def spread(blocks):
    size = lax.axis_size(DP)
    copies = jnp.broadcast_to(blocks[None], (size,) + blocks.shape)
    copies = copies.reshape((size * blocks.shape[0],) + blocks.shape[1:])
    whole = lax.all_to_all(copies, EVERY, split_axis=0, concat_axis=0, tiled=True)
    return whole.reshape((whole.shape[0] * whole.shape[1],) + whole.shape[2:])


def collect(parts):
    size, peers = lax.axis_size(DP), lax.axis_size("fsdp")
    blocks = parts.reshape((size * peers, parts.shape[0] // (size * peers)) + parts.shape[1:])
    blocks = lax.all_to_all(blocks, EVERY, split_axis=0, concat_axis=0, tiled=True)
    return jnp.sum(blocks.reshape((size, peers) + blocks.shape[1:]).astype(F32), axis=0)


def sum_scatter_pairs(blocks, axis):
    size = lax.axis_size(axis)
    if size & (size - 1):
        return jnp.sum(exchange(blocks).astype(F32), axis=0)
    index = lax.axis_index(axis)
    total = lax.dynamic_index_in_dim(blocks, index, 0, keepdims=False).astype(F32)
    for step in range(1, size):
        block = lax.dynamic_index_in_dim(blocks, index ^ step, 0, keepdims=False)
        total += lax.ppermute(block, axis, [(i, i ^ step) for i in range(size)]).astype(F32)
    return total


def zero_of(array):
    first = array[(0,) * array.ndim]
    return (first != first).astype(jnp.int32)


def after(array, other):
    return lax.dynamic_slice_in_dim(array, zero_of(other), array.shape[0], 0)


def gather_pairs(block, axis):
    size = lax.axis_size(axis)
    if size & (size - 1):
        return lax.all_gather(block, axis, axis=0, tiled=True)
    index = lax.axis_index(axis)
    step = 1
    while step < size:
        other = lax.ppermute(block, axis, [(i, i ^ step) for i in range(size)])
        second = (index & step) != 0
        block = jnp.concatenate(
            [jnp.where(second, other, block), jnp.where(second, block, other)], axis=0
        )
        step *= 2
    return block


def pad_lanes(array):
    short = -array.shape[-1] % LANES
    return jnp.pad(array, [(0, 0)] * (array.ndim - 1) + [(0, short)])


def body(
    tokens,
    segment,
    buckets,
    routes,
    w_query,
    w_key,
    w_value,
    w_output,
    w_router,
    norm_attn,
    norm_ffn,
    bias_table,
    expert_in,
    expert_out,
    out_grad,
):
    tok_rows, model = tokens.shape
    shard_rows = w_query.shape[0]
    peers = lax.axis_size("fsdp")
    group = tok_rows * peers
    capacity = 2 * tok_rows // peers
    heads = -(-HEADS // peers)
    own_cols = heads * HEAD
    all_cols = peers * own_cols
    me = lax.axis_index("fsdp")

    def by_peer(matrix):
        padded = jnp.pad(matrix, ((0, 0), (0, all_cols - HEADS * HEAD)))
        return jnp.transpose(padded.reshape(matrix.shape[0], peers, own_cols), (1, 0, 2))

    expert_pack = jnp.concatenate([expert_in[0].T, expert_out[0]], axis=1)

    rest = jnp.concatenate([w_router, norm_attn[:, None], norm_ffn[:, None]], axis=1)
    packed = pad_lanes(
        jnp.concatenate(
            [by_peer(w) for w in (w_query, w_key, w_value, w_output)]
            + [jnp.broadcast_to(rest[None], (peers,) + rest.shape)],
            axis=2,
        )
    )
    dense = spread(packed)
    qkv_cols = 3 * own_cols
    mat_cols = 4 * own_cols
    weight_qkv = dense[:, :qkv_cols]
    weight_router = dense[:, mat_cols : mat_cols + peers]
    gains = dense[:, mat_cols + peers : mat_cols + peers + 2].astype(F32).T
    gain_attn, gain_ffn = gains[0:1], gains[1:2]
    expert_weights = lax.all_gather(after(expert_pack, dense), "z", axis=0, tiled=True)
    output_blocks = gather_pairs(dense[:, qkv_cols:mat_cols], "fsdp").reshape(peers, model, own_cols)
    weight_output = jnp.transpose(output_blocks, (1, 0, 2)).reshape(model, all_cols)[:, :model]

    tokens_all = lax.all_gather(tokens, "fsdp", axis=0, tiled=True)
    segment_all = gather_pairs(segment, "fsdp")

    route = routes[:, 0]
    picked = (route[:, None] == jnp.arange(peers, dtype=jnp.int32)[None, :]).astype(jnp.int32)
    picked_float = picked.astype(F32)
    rank = jnp.sum((jnp.cumsum(picked, axis=0) - 1) * picked, axis=1)
    slot = route * capacity + rank
    slots = peers * capacity
    placing = (jnp.arange(slots, dtype=jnp.int32)[:, None] == slot[None, :]).astype(BF16)

    halves = lax.axis_size("y")

    def place_rows(rows):
        return product(placing, rows).astype(BF16).reshape(peers, capacity, rows.shape[-1])

    def dispatch(rows):
        placed = jnp.concatenate([place_rows(rows)] * halves, axis=0)
        placed = lax.all_to_all(placed, ("y", "fsdp"), split_axis=0, concat_axis=0, tiled=True)
        return placed.reshape(halves * slots, rows.shape[-1])

    def give_back(rows):
        blocks = rows.reshape(halves * peers, capacity, rows.shape[-1])
        blocks = lax.all_to_all(blocks, ("y", "fsdp"), split_axis=0, concat_axis=0, tiled=True)
        blocks = blocks.reshape(halves, slots, rows.shape[-1])
        whole = blocks[0]
        for half in range(1, halves):
            whole = (whole.astype(F32) + blocks[half].astype(F32)).astype(BF16)
        return contract(placing, 0, whole, 0)

    grad_arrived = dispatch(after(out_grad, dense))

    bucket_hot = (
        jnp.pad(buckets, (0, 1), constant_values=-1)[:, None]
        == jnp.arange(BUCKETS, dtype=jnp.int32)[None, :]
    )
    table_pad = jnp.pad(bias_table, ((0, 0), (0, peers * heads - HEADS)))
    own_table = lax.dynamic_slice_in_dim(table_pad, me * heads, heads, 1)
    offsets = contract(own_table, 0, bucket_hot.astype(BF16), 1)

    wide_all = tokens_all.astype(F32)
    unit_all = wide_all * inverse_rms(wide_all)
    hidden = (unit_all * gain_attn).astype(BF16)
    qkv, attended, probs = attend(
        offsets, segment_all, hidden, dense, ()
    )
    blocks = after(attended, grad_arrived).reshape(peers, tok_rows, own_cols)
    attn_out = jnp.transpose(exchange(blocks), (1, 0, 2)).reshape(tok_rows, all_cols)
    attn_out = attn_out[:, : HEADS * HEAD]

    inputs = tokens.astype(F32)
    residual = inputs + product(attn_out, weight_output)
    scale_ffn = inverse_rms(residual)
    unit_ffn = residual * scale_ffn
    hidden2 = (unit_ffn * gain_ffn).astype(BF16)
    logits = product(hidden2, weight_router)
    chances = jax.nn.softmax(logits, axis=-1)
    gate = jnp.sum(chances * picked_float, axis=-1, keepdims=True)

    gate_high = gate.astype(BF16)
    gate_low = (gate - gate_high.astype(F32)).astype(BF16)
    arrived = dispatch(pad_lanes(jnp.concatenate([hidden2, gate_high, gate_low], axis=1)))
    gate_slots = jnp.sum(arrived[:, model : model + 2].astype(F32), axis=1, keepdims=True)
    arrived = arrived[:, :model]
    d_arrived = (gate_slots * grad_arrived.astype(F32)).astype(BF16)
    result, activated, slopes = run_expert(arrived, expert_weights)
    token_result = give_back(result)
    d_rows, d_weights = run_expert_back(arrived, d_arrived, expert_weights, activated, slopes)
    d_expert = lax.psum_scatter(d_weights, "z", scatter_dimension=0, tiled=True).astype(F32)
    d_from_expert = give_back(d_rows)

    mixed = residual + gate * token_result
    grad_out = out_grad.astype(F32)
    d_gate = jnp.sum(grad_out * token_result, axis=-1, keepdims=True)
    d_logits = (gate * (picked_float - chances) * d_gate).astype(BF16)
    d_hidden2 = d_from_expert + contract(d_logits, 1, weight_router, 1)
    d_router = contract(hidden2, 0, d_logits, 0)
    d_gain_ffn = jnp.sum(d_hidden2 * unit_ffn, axis=0)
    d_residual = grad_out + norm_gradient(d_hidden2, gain_ffn, unit_ffn, scale_ffn)
    d_branch = d_residual.astype(BF16)
    d_weight_output = contract(attn_out, 0, d_branch, 0)
    d_attended = contract(d_branch, 1, weight_output, 1).astype(BF16)

    d_heads = exchange(by_peer(d_attended)).reshape(group, own_cols)
    d_qkv, d_offsets = attend_back(probs, d_heads, qkv, offsets.shape[-1], ())
    d_table = contract(bucket_hot.astype(F32), 0, d_offsets, 1, HIGHEST)
    d_table = lax.dynamic_update_slice_in_dim(
        jnp.zeros((BUCKETS, peers * heads), F32), d_table, me * heads, 1
    )
    d_hidden_part = contract(d_qkv, 0, weight_qkv, 1)
    d_gain_attn = jnp.sum(d_hidden_part * unit_all, axis=0)
    d_weight_qkv = contract(hidden, 0, d_qkv, 1)
    d_output_cols = exchange(by_peer(d_weight_output.astype(BF16)))
    d_output_cols = jnp.sum(d_output_cols.astype(F32), axis=0)
    d_rest = jnp.concatenate([d_router, d_gain_attn[:, None], d_gain_ffn[:, None]], axis=1)
    d_dense = jnp.concatenate(
        [
            pad_lanes(d_weight_qkv.astype(BF16)),
            pad_lanes(jnp.concatenate([d_output_cols.astype(BF16), d_rest.astype(BF16)], axis=1)),
        ],
        axis=1,
    )
    d_hidden = sum_scatter_pairs(
        d_hidden_part.astype(BF16).reshape(peers, tok_rows, model), "fsdp"
    )
    scale_attn = inverse_rms(inputs)
    d_inputs = d_residual + norm_gradient(d_hidden, gain_attn, inputs * scale_attn, scale_attn)
    table_total = total_everywhere(d_table)[:, :HEADS]
    d_own = collect(d_dense)
    output_first = qkv_cols + -qkv_cols % LANES
    rest_first = output_first + own_cols
    d_rest = jnp.sum(d_own[:, :, rest_first : rest_first + peers + 2], axis=0)

    def from_peers(first):
        cols = d_own[:, :, first : first + own_cols]
        return jnp.transpose(cols, (1, 0, 2)).reshape(shard_rows, all_cols)[:, : HEADS * HEAD]

    return (
        mixed.astype(BF16),
        d_inputs.astype(BF16),
        from_peers(0),
        from_peers(own_cols),
        from_peers(2 * own_cols),
        from_peers(output_first),
        d_rest[:, :peers],
        d_rest[:, peers],
        d_rest[:, peers + 1],
        table_total,
        d_expert[:, :model].T[None],
        d_expert[:, model:][None],
    )


def solution(mesh):
    dp, fsdp = mesh.shape["dp"], mesh.shape["fsdp"]
    pair = 2 if dp == 8 else 1
    mesh = jax.sharding.Mesh(mesh.devices.reshape(dp // pair, pair, fsdp), ("z", "y", "fsdp"))
    rows = P(("z", "y", "fsdp"), None)
    flat = P(("z", "y", "fsdp"))
    return jax.shard_map(
        body,
        mesh=mesh,
        in_specs=(
            rows,
            flat,
            P(),
            rows,
            rows,
            rows,
            rows,
            rows,
            rows,
            flat,
            flat,
            P(),
            P("fsdp", None, DP),
            P("fsdp", DP, None),
            rows,
        ),
        out_specs=(
            rows,
            rows,
            rows,
            rows,
            rows,
            rows,
            rows,
            flat,
            flat,
            P(),
            P("fsdp", None, DP),
            P("fsdp", DP, None),
        ),
        check_vma=False,
    )
```

```python
import functools

import jax
import jax.numpy as jnp
from jax import lax
from jax.experimental import pallas as pl
from jax.experimental.pallas import tpu as pltpu
from jax.sharding import PartitionSpec as P

HEADS = 12
HEAD = 64
BUCKETS = 32
LANES = 128
DP = ("z", "y")
EVERY = ("z", "y", "fsdp")
SUBLANES = 8

EPSILON = 1e-06
MASKED = -1000000000.0
HIGHEST = lax.Precision.HIGHEST
BF16 = jnp.bfloat16
F32 = jnp.float32


def inverse_rms(values):
    return lax.rsqrt(jnp.mean(values * values, axis=-1, keepdims=True) + EPSILON)


def norm_gradient(grad, gain, unit, scale):
    inner = grad * gain
    return scale * (inner - unit * jnp.mean(inner * unit, axis=-1, keepdims=True))


def product(left, right):
    return jnp.dot(left, right, preferred_element_type=F32)


def contract(left, left_dim, right, right_dim, precision=None):
    return lax.dot_general(
        left,
        right,
        (((left_dim,), (right_dim,)), ((), ())),
        precision=precision,
        preferred_element_type=F32,
    )


VMEM_LIMIT = 56 * 1024 * 1024


def head_slice(turn, heads, head):
    first = (turn * heads + head) * HEAD
    return slice(first, first + HEAD)


def attend_kernel(
    off_ref, seg_query_ref, seg_key_ref, hidden_ref, weight_ref, *refs, heads, waits
):
    qkv_ref, o_ref, p_ref, skew_ref = refs[waits:]
    turn = pl.program_id(0)
    rows = o_ref.shape[0]
    group = hidden_ref.shape[0]
    width = skew_ref.shape[2]

    @pl.when(turn == 0)
    def _():
        projected = product(hidden_ref[...], weight_ref[:, : 3 * heads * HEAD])
        qkv_ref[...] = projected.astype(BF16)
        for head in range(heads):
            wide = jnp.broadcast_to(off_ref[head : head + 1, :], (LANES, width))
            skew_ref[head] = pltpu.roll(wide, width - (LANES - 1), 1, stride=1, stride_axis=0)

    own_rows = pl.ds(pl.multiple_of(turn * rows, rows), rows)
    for head in range(heads):
        queries = qkv_ref[own_rows, head_slice(0, heads, head)]
        keys = qkv_ref[:, head_slice(1, heads, head)]
        values = qkv_ref[:, head_slice(2, heads, head)]
        scores = contract(queries, 1, keys, 1)
        for part in range(rows // LANES):
            here = slice(part * LANES, (part + 1) * LANES)
            start = group - LANES - turn * rows - part * LANES
            bias = skew_ref[head, :, pl.ds(pl.multiple_of(start, LANES), group)]
            keep = seg_query_ref[here, :] == seg_key_ref[...]
            biased = jnp.where(keep, scores[here] + bias, MASKED)
            top = jnp.max(biased, axis=1, keepdims=True)
            weights = jnp.exp(biased - top)
            total = jnp.sum(weights, axis=1, keepdims=True)
            probs = (weights * (1.0 / total)).astype(BF16)
            p_ref[head, here, :] = probs
            o_ref[here, head_slice(0, heads, head)] = product(probs, values).astype(BF16)


def attend_back_kernel(p_ref, do_ref, qkv_ref, *refs, heads, waits):
    dqkv_ref, doff_ref, dkv_acc, diag = refs[waits:]
    turn = pl.program_id(0)
    rows = do_ref.shape[0]
    group = qkv_ref.shape[0]
    width = diag.shape[2]

    @pl.when(turn == 0)
    def _():
        dkv_acc[...] = jnp.zeros_like(dkv_acc)
        diag[...] = jnp.zeros_like(diag)

    own_rows = pl.ds(pl.multiple_of(turn * rows, rows), rows)
    for head in range(heads):
        queries = qkv_ref[own_rows, head_slice(0, heads, head)]
        keys = qkv_ref[:, head_slice(1, heads, head)]
        values = qkv_ref[:, head_slice(2, heads, head)]
        probs = p_ref[head]
        grad = do_ref[:, head_slice(0, heads, head)]
        grad_probs = contract(grad, 1, values, 1)
        wide = probs.astype(F32)
        correction = jnp.sum(wide * grad_probs, axis=1, keepdims=True)
        grad_scores = (wide * (grad_probs - correction)).astype(BF16)
        dqkv_ref[head_slice(0, heads, head), own_rows] = product(grad_scores, keys).T.astype(BF16)
        dkv_acc[head_slice(0, heads, head), :] += contract(queries, 0, grad_scores, 0)
        dkv_acc[head_slice(1, heads, head), :] += contract(grad, 0, probs, 0)
        for part in range(rows // LANES):
            start = group - LANES - turn * rows - part * LANES
            there = pl.ds(pl.multiple_of(start, LANES), group)
            diag[head, :, there] += grad_scores[part * LANES : (part + 1) * LANES, :].astype(F32)

    @pl.when(turn == pl.num_programs(0) - 1)
    def _():
        dqkv_ref[heads * HEAD :, :] = dkv_acc[...].astype(BF16)
        for head in range(heads):
            lined = jnp.zeros((SUBLANES, width), F32)
            for first in range(0, LANES, SUBLANES):
                lined += pltpu.roll(diag[head, first : first + SUBLANES, :], LANES - 1 - first, 1)
            row = lax.broadcasted_iota(jnp.int32, lined.shape, 0)
            for bit in (1, 2, 4):
                lined = jnp.where((row & bit) != 0, pltpu.roll(lined, width - bit, 1), lined)
            doff_ref[head : head + 1, :] = jnp.sum(lined, axis=0, keepdims=True)


def whole_spec(array):
    return pl.BlockSpec(array.shape, lambda *_: (0,) * array.ndim)


def wait_specs(waits):
    return [pl.BlockSpec(memory_space=pl.ANY)] * len(waits)


def attend(offsets, segment, hidden, dense, waits):
    heads, width = offsets.shape
    group = hidden.shape[0]
    rows = min(256, group)
    own_cols = heads * HEAD
    operands = (offsets, segment[:, None], segment[None, :], hidden, dense)
    specs = [whole_spec(array) for array in operands]
    specs[1] = pl.BlockSpec((rows, 1), lambda b: (b, 0))
    return pl.pallas_call(
        functools.partial(attend_kernel, heads=heads, waits=len(waits)),
        grid=(group // rows,),
        in_specs=specs + wait_specs(waits),
        out_specs=[
            pl.BlockSpec((group, 3 * own_cols), lambda b: (0, 0)),
            pl.BlockSpec((rows, own_cols), lambda b: (b, 0)),
            pl.BlockSpec((heads, rows, group), lambda b: (0, b, 0)),
        ],
        out_shape=[
            jax.ShapeDtypeStruct((group, 3 * own_cols), BF16),
            jax.ShapeDtypeStruct((group, own_cols), BF16),
            jax.ShapeDtypeStruct((heads, group, group), BF16),
        ],
        scratch_shapes=[pltpu.VMEM((heads, LANES, width), F32)],
        compiler_params=pltpu.CompilerParams(vmem_limit_bytes=VMEM_LIMIT),
        cost_estimate=pl.CostEstimate(
            flops=80 * heads * group * group * HEAD,
            bytes_accessed=2 * heads * group * (group + 4 * HEAD),
            transcendentals=heads * group * group,
        ),
        name="attend",
    )(*operands, *waits)


def attend_back(probs, grads, qkv, width, waits):
    heads, group, _ = probs.shape
    rows = 512 if group == 1024 else min(256, group)
    own_cols = heads * HEAD
    return pl.pallas_call(
        functools.partial(attend_back_kernel, heads=heads, waits=len(waits)),
        grid=(group // rows,),
        in_specs=[
            pl.BlockSpec((heads, rows, group), lambda b: (0, b, 0)),
            pl.BlockSpec((rows, own_cols), lambda b: (b, 0)),
            whole_spec(qkv),
        ]
        + wait_specs(waits),
        out_specs=[
            pl.BlockSpec((3 * own_cols, group), lambda b: (0, 0)),
            pl.BlockSpec((heads, width), lambda b: (0, 0)),
        ],
        out_shape=[
            jax.ShapeDtypeStruct((3 * own_cols, group), BF16),
            jax.ShapeDtypeStruct((heads, width), F32),
        ],
        scratch_shapes=[
            pltpu.VMEM((2 * own_cols, group), F32),
            pltpu.VMEM((heads, LANES, width), F32),
        ],
        compiler_params=pltpu.CompilerParams(vmem_limit_bytes=VMEM_LIMIT),
        cost_estimate=pl.CostEstimate(
            flops=80 * heads * group * group * HEAD,
            bytes_accessed=2 * heads * group * (group + 8 * HEAD),
            transcendentals=0,
        ),
        name="attend_back",
    )(probs, grads, qkv, *waits)


GELU_SLOPE = 0.7978845608028654
GELU_CUBE = 0.044715


def expert_kernel(rows_ref, weights_ref, result_ref, act_ref, slope_ref, acc):
    turn = pl.program_id(0)
    model = rows_ref.shape[1]

    @pl.when(turn == 0)
    def _():
        acc[...] = jnp.zeros_like(acc)

    pre = contract(rows_ref[...], 1, weights_ref[:, :model], 1)
    square = pre * pre
    bend = jnp.tanh(GELU_SLOPE * pre * (1.0 + GELU_CUBE * square))
    half = 0.5 * (1.0 + bend)
    activated = (pre * half).astype(BF16)
    slope = half + 0.5 * GELU_SLOPE * pre * (1.0 - bend * bend) * (1.0 + 3.0 * GELU_CUBE * square)
    act_ref[...] = activated
    slope_ref[...] = slope.astype(BF16)
    acc[...] += product(activated, weights_ref[:, model:])

    @pl.when(turn == pl.num_programs(0) - 1)
    def _():
        result_ref[...] = acc[...].astype(BF16)


def expert_back_kernel(
    rows_ref, grads_ref, weights_ref, act_ref, slope_ref, back_ref, dw_ref, acc
):
    turn = pl.program_id(0)
    model = rows_ref.shape[1]

    @pl.when(turn == 0)
    def _():
        acc[...] = jnp.zeros_like(acc)

    rows, grads = rows_ref[...], grads_ref[...]
    d_act = contract(grads, 1, weights_ref[:, model:], 1)
    d_pre = (slope_ref[...].astype(F32) * d_act).astype(BF16)
    acc[...] += product(d_pre, weights_ref[:, :model])
    dw_ref[:, :model] = contract(d_pre, 0, rows, 0).astype(BF16)
    dw_ref[:, model:] = contract(act_ref[...], 0, grads, 0).astype(BF16)

    @pl.when(turn == pl.num_programs(0) - 1)
    def _():
        back_ref[...] = acc[...].astype(BF16)


def expert_cost(slot_rows, model, units, products):
    return pl.CostEstimate(
        flops=5 * products * slot_rows * model * units,
        bytes_accessed=4 * units * (model + slot_rows),
        transcendentals=0,
    )


def run_expert(rows, weights):
    slot_rows, model = rows.shape
    units, width = weights.shape
    step = 768 if units % 768 == 0 else units
    block = pl.BlockSpec((step, width), lambda i: (i, 0))
    across = pl.BlockSpec((slot_rows, step), lambda i: (0, i))
    hidden = jax.ShapeDtypeStruct((slot_rows, units), BF16)
    return pl.pallas_call(
        expert_kernel,
        grid=(units // step,),
        in_specs=[whole_spec(rows), block],
        out_specs=[whole_spec(rows), across, across],
        out_shape=[jax.ShapeDtypeStruct(rows.shape, BF16), hidden, hidden],
        scratch_shapes=[pltpu.VMEM(rows.shape, F32)],
        compiler_params=pltpu.CompilerParams(vmem_limit_bytes=VMEM_LIMIT),
        cost_estimate=expert_cost(slot_rows, model, units, 3),
        name="run_expert",
    )(rows, weights)


def run_expert_back(rows, grads, weights, activated, slopes):
    slot_rows, model = rows.shape
    units, width = weights.shape
    step = min(384, units)
    block = pl.BlockSpec((step, width), lambda i: (i, 0))
    across = pl.BlockSpec((slot_rows, step), lambda i: (0, i))
    return pl.pallas_call(
        expert_back_kernel,
        grid=(units // step,),
        in_specs=[whole_spec(rows), whole_spec(grads), block, across, across],
        out_specs=[whole_spec(rows), block],
        out_shape=[
            jax.ShapeDtypeStruct(rows.shape, BF16),
            jax.ShapeDtypeStruct((units, width), BF16),
        ],
        scratch_shapes=[pltpu.VMEM(rows.shape, F32)],
        compiler_params=pltpu.CompilerParams(vmem_limit_bytes=VMEM_LIMIT),
        cost_estimate=expert_cost(slot_rows, model, units, 4),
        name="run_expert_back",
    )(rows, grads, weights, activated, slopes)


def exchange(blocks):
    return lax.all_to_all(blocks, "fsdp", split_axis=0, concat_axis=0, tiled=True)


def total_everywhere(part):
    for axis in ("fsdp", "y", "z"):
        size = lax.axis_size(axis)
        step = 1
        while step < size:
            part = part + lax.ppermute(part, axis, [(i, i ^ step) for i in range(size)])
            step *= 2
    return part


def spread(blocks):
    size = lax.axis_size(DP)
    copies = jnp.broadcast_to(blocks[None], (size,) + blocks.shape)
    copies = copies.reshape((size * blocks.shape[0],) + blocks.shape[1:])
    whole = lax.all_to_all(copies, EVERY, split_axis=0, concat_axis=0, tiled=True)
    return whole.reshape((whole.shape[0] * whole.shape[1],) + whole.shape[2:])


def collect(parts):
    size, peers = lax.axis_size(DP), lax.axis_size("fsdp")
    blocks = parts.reshape((size * peers, parts.shape[0] // (size * peers)) + parts.shape[1:])
    blocks = lax.all_to_all(blocks, EVERY, split_axis=0, concat_axis=0, tiled=True)
    return jnp.sum(blocks.reshape((size, peers) + blocks.shape[1:]).astype(F32), axis=0)


def sum_scatter_pairs(blocks, axis):
    size = lax.axis_size(axis)
    if size & (size - 1):
        return jnp.sum(exchange(blocks).astype(F32), axis=0)
    index = lax.axis_index(axis)
    total = lax.dynamic_index_in_dim(blocks, index, 0, keepdims=False).astype(F32)
    for step in range(1, size):
        block = lax.dynamic_index_in_dim(blocks, index ^ step, 0, keepdims=False)
        total += lax.ppermute(block, axis, [(i, i ^ step) for i in range(size)]).astype(F32)
    return total


def after(array, other):
    first = other[(0,) * other.ndim]
    return jnp.where(first == first, array, jnp.zeros_like(array))


def gather_pairs(block, axis):
    size = lax.axis_size(axis)
    if size & (size - 1):
        return lax.all_gather(block, axis, axis=0, tiled=True)
    index = lax.axis_index(axis)
    step = 1
    while step < size:
        other = lax.ppermute(block, axis, [(i, i ^ step) for i in range(size)])
        second = (index & step) != 0
        block = jnp.concatenate(
            [jnp.where(second, other, block), jnp.where(second, block, other)], axis=0
        )
        step *= 2
    return block


def pad_lanes(array):
    short = -array.shape[-1] % LANES
    return jnp.pad(array, [(0, 0)] * (array.ndim - 1) + [(0, short)])


def body(
    tokens,
    segment,
    buckets,
    routes,
    w_query,
    w_key,
    w_value,
    w_output,
    w_router,
    norm_attn,
    norm_ffn,
    bias_table,
    expert_in,
    expert_out,
    out_grad,
):
    tok_rows, model = tokens.shape
    shard_rows = w_query.shape[0]
    peers = lax.axis_size("fsdp")
    group = tok_rows * peers
    capacity = 2 * tok_rows // peers
    heads = -(-HEADS // peers)
    own_cols = heads * HEAD
    all_cols = peers * own_cols
    me = lax.axis_index("fsdp")

    def by_peer(matrix):
        padded = jnp.pad(matrix, ((0, 0), (0, all_cols - HEADS * HEAD)))
        return jnp.transpose(padded.reshape(matrix.shape[0], peers, own_cols), (1, 0, 2))

    tokens_all = lax.all_gather(tokens, "fsdp", axis=0, tiled=True)

    expert_pack = jnp.concatenate([expert_in[0].T, expert_out[0]], axis=1)

    rest = jnp.concatenate([w_router, norm_attn[:, None], norm_ffn[:, None]], axis=1)
    packed = pad_lanes(
        jnp.concatenate(
            [by_peer(w) for w in (w_query, w_key, w_value, w_output)]
            + [jnp.broadcast_to(rest[None], (peers,) + rest.shape)],
            axis=2,
        )
    )
    dense = spread(packed)
    qkv_cols = 3 * own_cols
    mat_cols = 4 * own_cols
    weight_qkv = dense[:, :qkv_cols]
    weight_router = dense[:, mat_cols : mat_cols + peers]
    gains = dense[:, mat_cols + peers : mat_cols + peers + 2].astype(F32).T
    gain_attn, gain_ffn = gains[0:1], gains[1:2]
    expert_weights = lax.all_gather(after(expert_pack, tokens_all), "z", axis=0, tiled=True)
    output_blocks = gather_pairs(dense[:, qkv_cols:mat_cols], "fsdp").reshape(peers, model, own_cols)
    weight_output = jnp.transpose(output_blocks, (1, 0, 2)).reshape(model, all_cols)[:, :model]

    segment_all = gather_pairs(segment, "fsdp")

    route = routes[:, 0]
    picked = (route[:, None] == jnp.arange(peers, dtype=jnp.int32)[None, :]).astype(jnp.int32)
    picked_float = picked.astype(F32)
    rank = jnp.sum((jnp.cumsum(picked, axis=0) - 1) * picked, axis=1)
    slot = route * capacity + rank
    slots = peers * capacity
    placing = (jnp.arange(slots, dtype=jnp.int32)[:, None] == slot[None, :]).astype(BF16)

    halves = lax.axis_size("y")

    def place_rows(rows):
        return product(placing, rows).astype(BF16).reshape(peers, capacity, rows.shape[-1])

    def dispatch(rows):
        placed = jnp.concatenate([place_rows(rows)] * halves, axis=0)
        placed = lax.all_to_all(placed, ("y", "fsdp"), split_axis=0, concat_axis=0, tiled=True)
        return placed.reshape(halves * slots, rows.shape[-1])

    def give_back(rows):
        blocks = rows.reshape(halves * peers, capacity, rows.shape[-1])
        blocks = lax.all_to_all(blocks, ("y", "fsdp"), split_axis=0, concat_axis=0, tiled=True)
        blocks = blocks.reshape(halves, slots, rows.shape[-1])
        whole = blocks[0]
        for half in range(1, halves):
            whole = (whole.astype(F32) + blocks[half].astype(F32)).astype(BF16)
        return contract(placing, 0, whole, 0)

    grad_arrived = dispatch(after(out_grad, dense))

    bucket_hot = (
        jnp.pad(buckets, (0, 1), constant_values=-1)[:, None]
        == jnp.arange(BUCKETS, dtype=jnp.int32)[None, :]
    )
    table_pad = jnp.pad(bias_table, ((0, 0), (0, peers * heads - HEADS)))
    own_table = lax.dynamic_slice_in_dim(table_pad, me * heads, heads, 1)
    offsets = contract(own_table, 0, bucket_hot.astype(BF16), 1)

    wide_all = tokens_all.astype(F32)
    unit_all = wide_all * inverse_rms(wide_all)
    hidden = (unit_all * gain_attn).astype(BF16)
    qkv, attended, probs = attend(
        offsets, segment_all, hidden, dense, ()
    )
    blocks = attended.reshape(peers, tok_rows, own_cols)
    attn_out = jnp.transpose(exchange(blocks), (1, 0, 2)).reshape(tok_rows, all_cols)
    attn_out = attn_out[:, : HEADS * HEAD]

    inputs = tokens.astype(F32)
    residual = inputs + product(attn_out, weight_output)
    scale_ffn = inverse_rms(residual)
    unit_ffn = residual * scale_ffn
    hidden2 = (unit_ffn * gain_ffn).astype(BF16)
    logits = product(hidden2, weight_router)
    chances = jax.nn.softmax(logits, axis=-1)
    gate = jnp.sum(chances * picked_float, axis=-1, keepdims=True)

    gate_high = gate.astype(BF16)
    gate_low = (gate - gate_high.astype(F32)).astype(BF16)
    arrived = dispatch(pad_lanes(jnp.concatenate([hidden2, gate_high, gate_low], axis=1)))
    gate_slots = jnp.sum(arrived[:, model : model + 2].astype(F32), axis=1, keepdims=True)
    arrived = arrived[:, :model]
    d_arrived = (gate_slots * grad_arrived.astype(F32)).astype(BF16)
    result, activated, slopes = run_expert(arrived, expert_weights)
    token_result = give_back(result)
    d_rows, d_weights = run_expert_back(arrived, d_arrived, expert_weights, activated, slopes)
    d_expert = lax.psum_scatter(d_weights, "z", scatter_dimension=0, tiled=True).astype(F32)
    d_from_expert = give_back(d_rows)

    mixed = residual + gate * token_result
    grad_out = out_grad.astype(F32)
    d_gate = jnp.sum(grad_out * token_result, axis=-1, keepdims=True)
    d_logits = (gate * (picked_float - chances) * d_gate).astype(BF16)
    d_hidden2 = d_from_expert + contract(d_logits, 1, weight_router, 1)
    d_router = contract(hidden2, 0, d_logits, 0)
    d_gain_ffn = jnp.sum(d_hidden2 * unit_ffn, axis=0)
    d_residual = grad_out + norm_gradient(d_hidden2, gain_ffn, unit_ffn, scale_ffn)
    d_branch = d_residual.astype(BF16)
    d_weight_output = contract(attn_out, 0, d_branch, 0)
    d_attended = contract(d_branch, 1, weight_output, 1).astype(BF16)

    d_heads = exchange(by_peer(d_attended)).reshape(group, own_cols)
    d_qkv, d_offsets = attend_back(probs, d_heads, qkv, offsets.shape[-1], ())
    d_table = contract(bucket_hot.astype(F32), 0, d_offsets, 1, HIGHEST)
    d_table = lax.dynamic_update_slice_in_dim(
        jnp.zeros((BUCKETS, peers * heads), F32), d_table, me * heads, 1
    )
    d_weight_qkv = contract(hidden, 0, d_qkv, 1)
    d_output_cols = exchange(by_peer(d_weight_output.astype(BF16)))
    d_output_cols = jnp.sum(d_output_cols.astype(F32), axis=0)
    d_rest = jnp.concatenate([d_router, d_gain_ffn[:, None]], axis=1)
    d_dense = jnp.concatenate(
        [
            pad_lanes(d_weight_qkv.astype(BF16)),
            pad_lanes(jnp.concatenate([d_output_cols.astype(BF16), d_rest.astype(BF16)], axis=1)),
        ],
        axis=1,
    )
    d_hidden_part = contract(after(d_qkv, d_dense), 0, weight_qkv, 1)
    d_gain_attn = jnp.sum(d_hidden_part * unit_all, axis=0)
    d_hidden = sum_scatter_pairs(
        d_hidden_part.astype(BF16).reshape(peers, tok_rows, model), "fsdp"
    )
    scale_attn = inverse_rms(inputs)
    d_inputs = d_residual + norm_gradient(d_hidden, gain_attn, inputs * scale_attn, scale_attn)
    small = jnp.concatenate([d_table.reshape(-1), d_gain_attn])
    small = total_everywhere(pad_lanes(small[None]))[0]
    table_total = small[: d_table.size].reshape(d_table.shape)[:, :HEADS]
    own_first = lax.axis_index(EVERY) * shard_rows
    d_gain_attn = lax.dynamic_slice_in_dim(small, d_table.size + own_first, shard_rows, 0)
    d_own = collect(d_dense)
    output_first = qkv_cols + -qkv_cols % LANES
    rest_first = output_first + own_cols
    d_rest = jnp.sum(d_own[:, :, rest_first : rest_first + peers + 1], axis=0)

    def from_peers(first):
        cols = d_own[:, :, first : first + own_cols]
        return jnp.transpose(cols, (1, 0, 2)).reshape(shard_rows, all_cols)[:, : HEADS * HEAD]

    return (
        mixed.astype(BF16),
        d_inputs.astype(BF16),
        from_peers(0),
        from_peers(own_cols),
        from_peers(2 * own_cols),
        from_peers(output_first),
        d_rest[:, :peers],
        d_gain_attn,
        d_rest[:, peers],
        table_total,
        d_expert[:, :model].T[None],
        d_expert[:, model:][None],
    )


def solution(mesh):
    dp, fsdp = mesh.shape["dp"], mesh.shape["fsdp"]
    pair = 2 if dp == 8 else 1
    mesh = jax.sharding.Mesh(mesh.devices.reshape(dp // pair, pair, fsdp), ("z", "y", "fsdp"))
    rows = P(("z", "y", "fsdp"), None)
    flat = P(("z", "y", "fsdp"))
    return jax.shard_map(
        body,
        mesh=mesh,
        in_specs=(
            rows,
            flat,
            P(),
            rows,
            rows,
            rows,
            rows,
            rows,
            rows,
            flat,
            flat,
            P(),
            P("fsdp", None, DP),
            P("fsdp", DP, None),
            rows,
        ),
        out_specs=(
            rows,
            rows,
            rows,
            rows,
            rows,
            rows,
            rows,
            flat,
            flat,
            P(),
            P("fsdp", None, DP),
            P("fsdp", DP, None),
        ),
        check_vma=False,
    )
```

```python
import functools

import jax
import jax.numpy as jnp
from jax import lax
from jax.experimental import pallas as pl
from jax.experimental.pallas import tpu as pltpu
from jax.sharding import PartitionSpec as P

HEADS = 12
HEAD = 64
BUCKETS = 32
LANES = 128
DP = ("z", "y")
EVERY = ("z", "y", "fsdp")
SUBLANES = 8

EPSILON = 1e-06
MASKED = -1000000000.0
HIGHEST = lax.Precision.HIGHEST
BF16 = jnp.bfloat16
F32 = jnp.float32


def inverse_rms(values):
    return lax.rsqrt(jnp.mean(values * values, axis=-1, keepdims=True) + EPSILON)


def norm_gradient(grad, gain, unit, scale):
    inner = grad * gain
    return scale * (inner - unit * jnp.mean(inner * unit, axis=-1, keepdims=True))


def product(left, right):
    return jnp.dot(left, right, preferred_element_type=F32)


def contract(left, left_dim, right, right_dim, precision=None):
    return lax.dot_general(
        left,
        right,
        (((left_dim,), (right_dim,)), ((), ())),
        precision=precision,
        preferred_element_type=F32,
    )


VMEM_LIMIT = 56 * 1024 * 1024


def head_slice(turn, heads, head):
    first = (turn * heads + head) * HEAD
    return slice(first, first + HEAD)


def attend_kernel(
    off_ref, seg_query_ref, seg_key_ref, hidden_ref, weight_ref, *refs, heads, waits
):
    qkv_ref, o_ref, p_ref, skew_ref = refs[waits:]
    turn = pl.program_id(0)
    rows = o_ref.shape[0]
    group = hidden_ref.shape[0]
    width = skew_ref.shape[2]

    @pl.when(turn == 0)
    def _():
        projected = product(hidden_ref[...], weight_ref[:, : 3 * heads * HEAD])
        qkv_ref[...] = projected.astype(BF16)
        for head in range(heads):
            wide = jnp.broadcast_to(off_ref[head : head + 1, :], (LANES, width))
            skew_ref[head] = pltpu.roll(wide, width - (LANES - 1), 1, stride=1, stride_axis=0)

    own_rows = pl.ds(pl.multiple_of(turn * rows, rows), rows)
    for head in range(heads):
        queries = qkv_ref[own_rows, head_slice(0, heads, head)]
        keys = qkv_ref[:, head_slice(1, heads, head)]
        values = qkv_ref[:, head_slice(2, heads, head)]
        scores = contract(queries, 1, keys, 1)
        for part in range(rows // LANES):
            here = slice(part * LANES, (part + 1) * LANES)
            start = group - LANES - turn * rows - part * LANES
            bias = skew_ref[head, :, pl.ds(pl.multiple_of(start, LANES), group)]
            keep = seg_query_ref[here, :] == seg_key_ref[...]
            biased = jnp.where(keep, scores[here] + bias, MASKED)
            top = jnp.max(biased, axis=1, keepdims=True)
            weights = jnp.exp(biased - top)
            total = jnp.sum(weights, axis=1, keepdims=True)
            probs = (weights * (1.0 / total)).astype(BF16)
            p_ref[head, here, :] = probs
            o_ref[here, head_slice(0, heads, head)] = product(probs, values).astype(BF16)


def attend_back_kernel(p_ref, do_ref, qkv_ref, *refs, heads, waits):
    dqkv_ref, doff_ref, dkv_acc, diag = refs[waits:]
    turn = pl.program_id(0)
    rows = do_ref.shape[0]
    group = qkv_ref.shape[0]
    width = diag.shape[2]

    @pl.when(turn == 0)
    def _():
        dkv_acc[...] = jnp.zeros_like(dkv_acc)
        diag[...] = jnp.zeros_like(diag)

    own_rows = pl.ds(pl.multiple_of(turn * rows, rows), rows)
    for head in range(heads):
        queries = qkv_ref[own_rows, head_slice(0, heads, head)]
        keys = qkv_ref[:, head_slice(1, heads, head)]
        values = qkv_ref[:, head_slice(2, heads, head)]
        probs = p_ref[head]
        grad = do_ref[:, head_slice(0, heads, head)]
        grad_probs = contract(grad, 1, values, 1)
        wide = probs.astype(F32)
        correction = jnp.sum(wide * grad_probs, axis=1, keepdims=True)
        grad_scores = (wide * (grad_probs - correction)).astype(BF16)
        dqkv_ref[head_slice(0, heads, head), own_rows] = product(grad_scores, keys).T.astype(BF16)
        dkv_acc[head_slice(0, heads, head), :] += contract(queries, 0, grad_scores, 0)
        dkv_acc[head_slice(1, heads, head), :] += contract(grad, 0, probs, 0)
        for part in range(rows // LANES):
            start = group - LANES - turn * rows - part * LANES
            there = pl.ds(pl.multiple_of(start, LANES), group)
            diag[head, :, there] += grad_scores[part * LANES : (part + 1) * LANES, :].astype(F32)

    @pl.when(turn == pl.num_programs(0) - 1)
    def _():
        dqkv_ref[heads * HEAD :, :] = dkv_acc[...].astype(BF16)
        for head in range(heads):
            lined = jnp.zeros((SUBLANES, width), F32)
            for first in range(0, LANES, SUBLANES):
                lined += pltpu.roll(diag[head, first : first + SUBLANES, :], LANES - 1 - first, 1)
            row = lax.broadcasted_iota(jnp.int32, lined.shape, 0)
            for bit in (1, 2, 4):
                lined = jnp.where((row & bit) != 0, pltpu.roll(lined, width - bit, 1), lined)
            doff_ref[head : head + 1, :] = jnp.sum(lined, axis=0, keepdims=True)


def whole_spec(array):
    return pl.BlockSpec(array.shape, lambda *_: (0,) * array.ndim)


def wait_specs(waits):
    return [pl.BlockSpec(memory_space=pl.ANY)] * len(waits)


def attend(offsets, segment, hidden, dense, waits):
    heads, width = offsets.shape
    group = hidden.shape[0]
    rows = min(256, group)
    own_cols = heads * HEAD
    operands = (offsets, segment[:, None], segment[None, :], hidden, dense)
    specs = [whole_spec(array) for array in operands]
    specs[1] = pl.BlockSpec((rows, 1), lambda b: (b, 0))
    return pl.pallas_call(
        functools.partial(attend_kernel, heads=heads, waits=len(waits)),
        grid=(group // rows,),
        in_specs=specs + wait_specs(waits),
        out_specs=[
            pl.BlockSpec((group, 3 * own_cols), lambda b: (0, 0)),
            pl.BlockSpec((rows, own_cols), lambda b: (b, 0)),
            pl.BlockSpec((heads, rows, group), lambda b: (0, b, 0)),
        ],
        out_shape=[
            jax.ShapeDtypeStruct((group, 3 * own_cols), BF16),
            jax.ShapeDtypeStruct((group, own_cols), BF16),
            jax.ShapeDtypeStruct((heads, group, group), BF16),
        ],
        scratch_shapes=[pltpu.VMEM((heads, LANES, width), F32)],
        compiler_params=pltpu.CompilerParams(vmem_limit_bytes=VMEM_LIMIT),
        cost_estimate=pl.CostEstimate(
            flops=80 * heads * group * group * HEAD,
            bytes_accessed=2 * heads * group * (group + 4 * HEAD),
            transcendentals=heads * group * group,
        ),
        name="attend",
    )(*operands, *waits)


def attend_back(probs, grads, qkv, width, waits):
    heads, group, _ = probs.shape
    rows = 512 if group == 1024 else min(256, group)
    own_cols = heads * HEAD
    return pl.pallas_call(
        functools.partial(attend_back_kernel, heads=heads, waits=len(waits)),
        grid=(group // rows,),
        in_specs=[
            pl.BlockSpec((heads, rows, group), lambda b: (0, b, 0)),
            pl.BlockSpec((rows, own_cols), lambda b: (b, 0)),
            whole_spec(qkv),
        ]
        + wait_specs(waits),
        out_specs=[
            pl.BlockSpec((3 * own_cols, group), lambda b: (0, 0)),
            pl.BlockSpec((heads, width), lambda b: (0, 0)),
        ],
        out_shape=[
            jax.ShapeDtypeStruct((3 * own_cols, group), BF16),
            jax.ShapeDtypeStruct((heads, width), F32),
        ],
        scratch_shapes=[
            pltpu.VMEM((2 * own_cols, group), F32),
            pltpu.VMEM((heads, LANES, width), F32),
        ],
        compiler_params=pltpu.CompilerParams(vmem_limit_bytes=VMEM_LIMIT),
        cost_estimate=pl.CostEstimate(
            flops=80 * heads * group * group * HEAD,
            bytes_accessed=2 * heads * group * (group + 8 * HEAD),
            transcendentals=0,
        ),
        name="attend_back",
    )(probs, grads, qkv, *waits)


GELU_SLOPE = 0.7978845608028654
GELU_CUBE = 0.044715


def expert_kernel(rows_ref, weights_ref, result_ref, act_ref, slope_ref, acc):
    turn = pl.program_id(0)
    model = rows_ref.shape[1]

    @pl.when(turn == 0)
    def _():
        acc[...] = jnp.zeros_like(acc)

    pre = contract(rows_ref[...], 1, weights_ref[:, :model], 1)
    square = pre * pre
    bend = jnp.tanh(GELU_SLOPE * pre * (1.0 + GELU_CUBE * square))
    half = 0.5 * (1.0 + bend)
    activated = (pre * half).astype(BF16)
    slope = half + 0.5 * GELU_SLOPE * pre * (1.0 - bend * bend) * (1.0 + 3.0 * GELU_CUBE * square)
    act_ref[...] = activated
    slope_ref[...] = slope.astype(BF16)
    acc[...] += product(activated, weights_ref[:, model:])

    @pl.when(turn == pl.num_programs(0) - 1)
    def _():
        result_ref[...] = acc[...].astype(BF16)


def expert_back_kernel(
    rows_ref, grads_ref, weights_ref, act_ref, slope_ref, back_ref, dw_ref, acc
):
    turn = pl.program_id(0)
    model = rows_ref.shape[1]

    @pl.when(turn == 0)
    def _():
        acc[...] = jnp.zeros_like(acc)

    rows, grads = rows_ref[...], grads_ref[...]
    d_act = contract(grads, 1, weights_ref[:, model:], 1)
    d_pre = (slope_ref[...].astype(F32) * d_act).astype(BF16)
    acc[...] += product(d_pre, weights_ref[:, :model])
    dw_ref[:, :model] = contract(d_pre, 0, rows, 0).astype(BF16)
    dw_ref[:, model:] = contract(act_ref[...], 0, grads, 0).astype(BF16)

    @pl.when(turn == pl.num_programs(0) - 1)
    def _():
        back_ref[...] = acc[...].astype(BF16)


def expert_cost(slot_rows, model, units, products):
    return pl.CostEstimate(
        flops=5 * products * slot_rows * model * units,
        bytes_accessed=4 * units * (model + slot_rows),
        transcendentals=0,
    )


def run_expert(rows, weights):
    slot_rows, model = rows.shape
    units, width = weights.shape
    step = 768 if units % 768 == 0 else units
    block = pl.BlockSpec((step, width), lambda i: (i, 0))
    across = pl.BlockSpec((slot_rows, step), lambda i: (0, i))
    hidden = jax.ShapeDtypeStruct((slot_rows, units), BF16)
    return pl.pallas_call(
        expert_kernel,
        grid=(units // step,),
        in_specs=[whole_spec(rows), block],
        out_specs=[whole_spec(rows), across, across],
        out_shape=[jax.ShapeDtypeStruct(rows.shape, BF16), hidden, hidden],
        scratch_shapes=[pltpu.VMEM(rows.shape, F32)],
        compiler_params=pltpu.CompilerParams(vmem_limit_bytes=VMEM_LIMIT),
        cost_estimate=expert_cost(slot_rows, model, units, 3),
        name="run_expert",
    )(rows, weights)


def run_expert_back(rows, grads, weights, activated, slopes):
    slot_rows, model = rows.shape
    units, width = weights.shape
    step = min(384, units)
    block = pl.BlockSpec((step, width), lambda i: (i, 0))
    across = pl.BlockSpec((slot_rows, step), lambda i: (0, i))
    return pl.pallas_call(
        expert_back_kernel,
        grid=(units // step,),
        in_specs=[whole_spec(rows), whole_spec(grads), block, across, across],
        out_specs=[whole_spec(rows), block],
        out_shape=[
            jax.ShapeDtypeStruct(rows.shape, BF16),
            jax.ShapeDtypeStruct((units, width), BF16),
        ],
        scratch_shapes=[pltpu.VMEM(rows.shape, F32)],
        compiler_params=pltpu.CompilerParams(vmem_limit_bytes=VMEM_LIMIT),
        cost_estimate=expert_cost(slot_rows, model, units, 4),
        name="run_expert_back",
    )(rows, grads, weights, activated, slopes)


def exchange(blocks):
    return lax.all_to_all(blocks, "fsdp", split_axis=0, concat_axis=0, tiled=True)


def total_everywhere(part):
    for axis in ("fsdp", "y", "z"):
        size = lax.axis_size(axis)
        step = 1
        while step < size:
            part = part + lax.ppermute(part, axis, [(i, i ^ step) for i in range(size)])
            step *= 2
    return part


def spread(blocks):
    size = lax.axis_size(DP)
    copies = jnp.broadcast_to(blocks[None], (size,) + blocks.shape)
    copies = copies.reshape((size * blocks.shape[0],) + blocks.shape[1:])
    whole = lax.all_to_all(copies, EVERY, split_axis=0, concat_axis=0, tiled=True)
    return whole.reshape((whole.shape[0] * whole.shape[1],) + whole.shape[2:])


def collect(parts):
    size, peers = lax.axis_size(DP), lax.axis_size("fsdp")
    blocks = parts.reshape((size * peers, parts.shape[0] // (size * peers)) + parts.shape[1:])
    blocks = lax.all_to_all(blocks, EVERY, split_axis=0, concat_axis=0, tiled=True)
    return jnp.sum(blocks.reshape((size, peers) + blocks.shape[1:]).astype(F32), axis=0)


def sum_scatter_pairs(blocks, axis):
    size = lax.axis_size(axis)
    if size & (size - 1):
        return jnp.sum(exchange(blocks).astype(F32), axis=0)
    index = lax.axis_index(axis)
    total = lax.dynamic_index_in_dim(blocks, index, 0, keepdims=False).astype(F32)
    for step in range(1, size):
        block = lax.dynamic_index_in_dim(blocks, index ^ step, 0, keepdims=False)
        total += lax.ppermute(block, axis, [(i, i ^ step) for i in range(size)]).astype(F32)
    return total


def after(array, other):
    first = other[(0,) * other.ndim]
    return jnp.where(first == first, array, jnp.zeros_like(array))


def gather_pairs(block, axis):
    size = lax.axis_size(axis)
    if size & (size - 1):
        return lax.all_gather(block, axis, axis=0, tiled=True)
    index = lax.axis_index(axis)
    step = 1
    while step < size:
        other = lax.ppermute(block, axis, [(i, i ^ step) for i in range(size)])
        second = (index & step) != 0
        block = jnp.concatenate(
            [jnp.where(second, other, block), jnp.where(second, block, other)], axis=0
        )
        step *= 2
    return block


def pad_lanes(array):
    short = -array.shape[-1] % LANES
    return jnp.pad(array, [(0, 0)] * (array.ndim - 1) + [(0, short)])


def body(
    tokens,
    segment,
    buckets,
    routes,
    w_query,
    w_key,
    w_value,
    w_output,
    w_router,
    norm_attn,
    norm_ffn,
    bias_table,
    expert_in,
    expert_out,
    out_grad,
):
    tok_rows, model = tokens.shape
    shard_rows = w_query.shape[0]
    peers = lax.axis_size("fsdp")
    group = tok_rows * peers
    capacity = 2 * tok_rows // peers
    heads = -(-HEADS // peers)
    own_cols = heads * HEAD
    all_cols = peers * own_cols
    me = lax.axis_index("fsdp")

    def by_peer(matrix):
        padded = jnp.pad(matrix, ((0, 0), (0, all_cols - HEADS * HEAD)))
        return jnp.transpose(padded.reshape(matrix.shape[0], peers, own_cols), (1, 0, 2))

    tokens_all = lax.all_gather(tokens, "fsdp", axis=0, tiled=True)

    expert_pack = jnp.concatenate([expert_in[0].T, expert_out[0]], axis=1)

    rest = jnp.concatenate([w_router, norm_attn[:, None], norm_ffn[:, None]], axis=1)
    packed = pad_lanes(
        jnp.concatenate(
            [by_peer(w) for w in (w_query, w_key, w_value, w_output)]
            + [jnp.broadcast_to(rest[None], (peers,) + rest.shape)],
            axis=2,
        )
    )
    dense = spread(packed)
    qkv_cols = 3 * own_cols
    mat_cols = 4 * own_cols
    weight_qkv = dense[:, :qkv_cols]
    weight_router = dense[:, mat_cols : mat_cols + peers]
    gains = dense[:, mat_cols + peers : mat_cols + peers + 2].astype(F32).T
    gain_attn, gain_ffn = gains[0:1], gains[1:2]
    expert_weights = lax.all_gather(after(expert_pack, tokens_all), "z", axis=0, tiled=True)
    output_blocks = gather_pairs(dense[:, qkv_cols:mat_cols], "fsdp").reshape(peers, model, own_cols)
    weight_output = jnp.transpose(output_blocks, (1, 0, 2)).reshape(model, all_cols)[:, :model]

    segment_all = gather_pairs(segment, "fsdp")

    route = routes[:, 0]
    picked = (route[:, None] == jnp.arange(peers, dtype=jnp.int32)[None, :]).astype(jnp.int32)
    picked_float = picked.astype(F32)
    rank = jnp.sum((jnp.cumsum(picked, axis=0) - 1) * picked, axis=1)
    slot = route * capacity + rank
    slots = peers * capacity
    placing = (jnp.arange(slots, dtype=jnp.int32)[:, None] == slot[None, :]).astype(BF16)

    halves = lax.axis_size("y")

    def place_rows(rows):
        return product(placing, rows).astype(BF16).reshape(peers, capacity, rows.shape[-1])

    def dispatch(rows):
        placed = jnp.concatenate([place_rows(rows)] * halves, axis=0)
        placed = lax.all_to_all(placed, ("y", "fsdp"), split_axis=0, concat_axis=0, tiled=True)
        return placed.reshape(halves * slots, rows.shape[-1])

    def give_back(rows):
        blocks = rows.reshape(halves * peers, capacity, rows.shape[-1])
        blocks = lax.all_to_all(blocks, ("y", "fsdp"), split_axis=0, concat_axis=0, tiled=True)
        blocks = blocks.reshape(halves, slots, rows.shape[-1])
        whole = blocks[0]
        for half in range(1, halves):
            whole = (whole.astype(F32) + blocks[half].astype(F32)).astype(BF16)
        return contract(placing, 0, whole, 0)

    bucket_hot = (
        jnp.pad(buckets, (0, 1), constant_values=-1)[:, None]
        == jnp.arange(BUCKETS, dtype=jnp.int32)[None, :]
    )
    table_pad = jnp.pad(bias_table, ((0, 0), (0, peers * heads - HEADS)))
    own_table = lax.dynamic_slice_in_dim(table_pad, me * heads, heads, 1)
    offsets = contract(own_table, 0, bucket_hot.astype(BF16), 1)

    wide_all = tokens_all.astype(F32)
    unit_all = wide_all * inverse_rms(wide_all)
    hidden = (unit_all * gain_attn).astype(BF16)
    qkv, attended, probs = attend(
        offsets, segment_all, hidden, dense, ()
    )
    blocks = attended.reshape(peers, tok_rows, own_cols)
    attn_out = jnp.transpose(exchange(blocks), (1, 0, 2)).reshape(tok_rows, all_cols)
    attn_out = attn_out[:, : HEADS * HEAD]

    inputs = tokens.astype(F32)
    residual = inputs + product(attn_out, weight_output)
    scale_ffn = inverse_rms(residual)
    unit_ffn = residual * scale_ffn
    hidden2 = (unit_ffn * gain_ffn).astype(BF16)
    logits = product(hidden2, weight_router)
    chances = jax.nn.softmax(logits, axis=-1)
    gate = jnp.sum(chances * picked_float, axis=-1, keepdims=True)

    gate_high = gate.astype(BF16)
    gate_low = (gate - gate_high.astype(F32)).astype(BF16)
    arrived = dispatch(
        pad_lanes(jnp.concatenate([hidden2, out_grad, gate_high, gate_low], axis=1))
    )
    gate_slots = jnp.sum(arrived[:, 2 * model : 2 * model + 2].astype(F32), axis=1, keepdims=True)
    grad_arrived = arrived[:, model : 2 * model]
    arrived = arrived[:, :model]
    d_arrived = (gate_slots * grad_arrived.astype(F32)).astype(BF16)
    result, activated, slopes = run_expert(arrived, expert_weights)
    token_result = give_back(result)
    d_rows, d_weights = run_expert_back(arrived, d_arrived, expert_weights, activated, slopes)
    d_expert = lax.psum_scatter(d_weights, "z", scatter_dimension=0, tiled=True).astype(F32)
    d_from_expert = give_back(d_rows)

    mixed = residual + gate * token_result
    grad_out = out_grad.astype(F32)
    d_gate = jnp.sum(grad_out * token_result, axis=-1, keepdims=True)
    d_logits = (gate * (picked_float - chances) * d_gate).astype(BF16)
    d_hidden2 = d_from_expert + contract(d_logits, 1, weight_router, 1)
    d_router = contract(hidden2, 0, d_logits, 0)
    d_gain_ffn = jnp.sum(d_hidden2 * unit_ffn, axis=0)
    d_residual = grad_out + norm_gradient(d_hidden2, gain_ffn, unit_ffn, scale_ffn)
    d_branch = d_residual.astype(BF16)
    d_weight_output = contract(attn_out, 0, d_branch, 0)
    d_attended = contract(d_branch, 1, weight_output, 1).astype(BF16)

    d_heads = exchange(by_peer(d_attended)).reshape(group, own_cols)
    d_qkv, d_offsets = attend_back(probs, d_heads, qkv, offsets.shape[-1], ())
    d_table = contract(bucket_hot.astype(F32), 0, d_offsets, 1, HIGHEST)
    d_table = lax.dynamic_update_slice_in_dim(
        jnp.zeros((BUCKETS, peers * heads), F32), d_table, me * heads, 1
    )
    d_weight_qkv = contract(hidden, 0, d_qkv, 1)
    d_output_cols = exchange(by_peer(d_weight_output.astype(BF16)))
    d_output_cols = jnp.sum(d_output_cols.astype(F32), axis=0)
    d_rest = jnp.concatenate([d_router, d_gain_ffn[:, None]], axis=1)
    d_dense = jnp.concatenate(
        [
            pad_lanes(d_weight_qkv.astype(BF16)),
            pad_lanes(jnp.concatenate([d_output_cols.astype(BF16), d_rest.astype(BF16)], axis=1)),
        ],
        axis=1,
    )
    d_hidden_part = contract(after(d_qkv, d_dense), 0, weight_qkv, 1)
    d_gain_attn = jnp.sum(d_hidden_part * unit_all, axis=0)
    d_hidden = sum_scatter_pairs(
        d_hidden_part.astype(BF16).reshape(peers, tok_rows, model), "fsdp"
    )
    scale_attn = inverse_rms(inputs)
    d_inputs = d_residual + norm_gradient(d_hidden, gain_attn, inputs * scale_attn, scale_attn)
    small = jnp.concatenate([d_table.reshape(-1), d_gain_attn])
    small = total_everywhere(pad_lanes(small[None]))[0]
    table_total = small[: d_table.size].reshape(d_table.shape)[:, :HEADS]
    own_first = lax.axis_index(EVERY) * shard_rows
    d_gain_attn = lax.dynamic_slice_in_dim(small, d_table.size + own_first, shard_rows, 0)
    d_own = collect(d_dense)
    output_first = qkv_cols + -qkv_cols % LANES
    rest_first = output_first + own_cols
    d_rest = jnp.sum(d_own[:, :, rest_first : rest_first + peers + 1], axis=0)

    def from_peers(first):
        cols = d_own[:, :, first : first + own_cols]
        return jnp.transpose(cols, (1, 0, 2)).reshape(shard_rows, all_cols)[:, : HEADS * HEAD]

    return (
        mixed.astype(BF16),
        d_inputs.astype(BF16),
        from_peers(0),
        from_peers(own_cols),
        from_peers(2 * own_cols),
        from_peers(output_first),
        d_rest[:, :peers],
        d_gain_attn,
        d_rest[:, peers],
        table_total,
        d_expert[:, :model].T[None],
        d_expert[:, model:][None],
    )


def solution(mesh):
    dp, fsdp = mesh.shape["dp"], mesh.shape["fsdp"]
    pair = 2 if dp == 8 else 1
    mesh = jax.sharding.Mesh(mesh.devices.reshape(dp // pair, pair, fsdp), ("z", "y", "fsdp"))
    rows = P(("z", "y", "fsdp"), None)
    flat = P(("z", "y", "fsdp"))
    return jax.shard_map(
        body,
        mesh=mesh,
        in_specs=(
            rows,
            flat,
            P(),
            rows,
            rows,
            rows,
            rows,
            rows,
            rows,
            flat,
            flat,
            P(),
            P("fsdp", None, DP),
            P("fsdp", DP, None),
            rows,
        ),
        out_specs=(
            rows,
            rows,
            rows,
            rows,
            rows,
            rows,
            rows,
            flat,
            flat,
            P(),
            P("fsdp", None, DP),
            P("fsdp", DP, None),
        ),
        check_vma=False,
    )
```
